128 devices in a mesh: atm: 32 (over x, y, core), ocn: 4 (over z).
Axes of the slice: x: 4, y: 4, z: 4, core: 2. Of those that a mesh axis runs over, the one named last changes fastest.
Arguments:
- source_flux: bfloat16 [4, 262144], P(None, ('atm', 'ocn')), may hold values from -6 to 6
- remap_weights: bfloat16 [73728, 128, 128], P(('atm', 'ocn')), may hold values from -0.1875 to 0.1875
- source_block: int32 [73728], P(('atm', 'ocn')), may hold values from 0 to 15
- owner_device: int32 [73728, 1], P(('atm', 'ocn')), may hold values from 0 to 127; in each aligned block of 576 rows (0 to 575, 576 to 1151, ...) at most 9 rows name the same one
- target_row: int32 [73728], P(('atm', 'ocn')), may hold values from 0 to 63
- sea_height: float32 [2048, 512], P('atm', 'ocn'), may hold values from -6 to 6
- u_velocity: float32 [2048, 512], P('atm', 'ocn'), may hold values from -6 to 6
- v_velocity: float32 [2048, 512], P('atm', 'ocn'), may hold values from -6 to 6
- ocean_depth: float32 [2048, 512], P('atm', 'ocn'), may hold values from 0.5 to 2
Outputs:
- ocean_flux: float32 [4, 2048, 512], P(None, 'atm', 'ocn')
- height_next: float32 [2048, 512], P('atm', 'ocn')
- zonal_next: float32 [2048, 512], P('atm', 'ocn')
- merid_next: float32 [2048, 512], P('atm', 'ocn')
The draws below stay inside these ranges and needn't reach their ends.
Inputs may be any that keep to these rules, and one draw needn't show every extreme that they name: `owner_device`: among the 576 weight blocks of one device no owner is named more than 9 times, a bound that some block reaches.
All inputs are finite; a program needn't handle non-finite values.
Results may differ from the reference program's by a relative error of at most 0.0003.
Values sent between devices are 32-bit elements; how exact they have to be, the bound alone decides.
No kernel may reach another device: no remote copies, remote signals or barrier semaphores. Data moves between devices by JAX's collectives and lax.ppermute only.
A program may use at most 64 MiB of HBM per device.

```python
import math
import jax
import jax.numpy as jnp
import numpy as np
from jax import lax

F = 4
B = 128
SB = 16
NW = 576
CX = 64
STEPS = 3
CAP = 9
SRC = 262144
WBLOCKS = 73728
NX = 2048
NY = 512
N_ATM = 32
N_OCN = 4
DEVICES = 128


def touch_ends(result, stream_key, least, largest):
    longest = result.shape.index(max(result.shape))
    spots = []
    for shift in (0, 1):
        where = [jax.random.randint(jax.random.fold_in(stream_key, axis), (), 0, length) for axis, length in enumerate(result.shape)]
        where[longest] = (where[longest] + shift) % result.shape[longest]
        spots.append(tuple(where))
    return result.at[spots[0]].set(least).at[spots[1]].set(largest)


def level_of(rng, extent, shards, low, top_value):
    def one(dim, parts):
        draws = jax.random.uniform(jax.random.fold_in(jax.random.fold_in(rng, 6), dim), (parts,), jnp.float32, low / len(shards), top_value / len(shards))
        return jnp.repeat(jnp.exp(draws), extent[dim] // parts).reshape((-1,) + (1,) * (len(extent) - dim - 1))

    level = one(*shards[0])
    for cut in shards[1:]:
        level = level * one(*cut)
    return level


def routed_block(key, own, number, rows, count, top, bound, slope):
    ranking = jax.random.permutation(key, count)
    crowded, common = shares(count, rows * top, bound, slope, True), shares(count, rows * top, bound, slope, False)
    places = jnp.arange(count)

    def named(tallies, turn):
        used = int((tallies > 0).sum())
        fixed = max(1, used // 4)
        shifted = fixed + (places - fixed + turn * (used - fixed)) % max(1, count - fixed)
        return jnp.zeros((count,), jnp.int32).at[ranking[jnp.where(places < fixed, places, shifted)]].set(jnp.asarray(tallies, jnp.int32))

    tallies = jnp.where(number % 4 == 0, named(crowded, number // 4), named(common, number - number // 4 - 1))
    mixed = jax.random.permutation(jax.random.fold_in(own, 3), count)
    giver, receiver = mixed[0:count // 2 * 2:2], mixed[1:count // 2 * 2:2]
    room = jnp.minimum(tallies[giver] - 1, bound - tallies[receiver]) // 2
    room = jnp.where((giver == ranking[0]) | (receiver == ranking[0]) | (tallies[receiver] == 0), 0, jnp.maximum(room, 0))
    shifted = jax.random.randint(jax.random.fold_in(own, 4), (count // 2,), 0, 1 << 20) % (room + 1)
    tallies = tallies.at[giver].add(-shifted).at[receiver].add(shifted)
    members = jnp.searchsorted(jnp.cumsum(tallies), jnp.arange(rows * top), side="right").astype(jnp.int32)
    grid = members.reshape(top, rows).T
    grid = grid[jax.random.permutation(jax.random.fold_in(own, 1), rows)]
    turn = jax.random.randint(jax.random.fold_in(own, 2), (rows, 1), 0, top)
    return jnp.take_along_axis(grid, (jnp.arange(top)[None, :] + turn) % top, axis=1)


def shares(amount, total, most, lean, full):
    portions = [(1 << 20) // math.isqrt(rank ** lean) + 1 for rank in range(1, amount + 1)]
    largest = most if full else min(most, max(-(-total // amount), total * portions[0] // sum(portions)))
    least = 1 if total - largest >= amount - 1 else 0
    counts, spare = [largest] + [least] * (amount - 1), total - largest - least * (amount - 1)
    while spare > 0:
        free = [i for i in range(1, amount) if counts[i] < largest] or [i for i in range(1, amount) if counts[i] < most]
        whole, budget = sum([portions[i] for i in free]), spare
        for i in free:
            extra = min(most - counts[i], max(1, budget * portions[i] // whole), spare)
            counts[i] = counts[i] + extra
            spare = spare - extra
    return np.array(counts)


def scatter_about(own_key, dims, deviation, reach, shards=(), held_as=jnp.bfloat16):
    result = jax.random.normal(own_key, dims, jnp.float32) * deviation
    if len(shards) > 0:
        result = level_of(own_key, dims, shards, -0.22, 0.18) * result
    return jnp.clip(result, min=-reach, max=reach).astype(held_as)


def setup_inputs(seed: int = 0) -> dict:
    arg_keys = jax.random.split(jax.random.key(seed), 10)
    source_flux = scatter_about(arg_keys[0], (F, SRC), 1.0, 6.0, ((1, 128),))
    remap_weights = scatter_about(arg_keys[1], (WBLOCKS, B, B), (B * NW // CX) ** -0.5, 0.1875, ((0, 128),))
    source_block = touch_ends(jax.random.randint(arg_keys[2], (WBLOCKS,), 0, SB), jax.random.fold_in(arg_keys[2], 1), 0, SB - 1).astype(jnp.int32)
    owner_device_keys = jax.random.split(jax.random.fold_in(arg_keys[3], 1), WBLOCKS // NW)
    owner_device_turns = jax.random.permutation(jax.random.fold_in(arg_keys[3], 3), WBLOCKS // NW)
    owner_device = jax.vmap(lambda own, number: routed_block(jax.random.fold_in(arg_keys[3], 2), own, number, NW, DEVICES, 1, CAP, 2))(owner_device_keys, owner_device_turns).reshape((WBLOCKS, 1))
    target_row = touch_ends(jax.random.randint(arg_keys[4], (WBLOCKS,), 0, CX), jax.random.fold_in(arg_keys[4], 1), 0, CX - 1).astype(jnp.int32)
    sea_height = scatter_about(arg_keys[5], (NX, NY), 1.0, 6.0, ((0, 32), (1, 4)), jnp.float32)
    u_velocity = scatter_about(arg_keys[6], (NX, NY), 1.0, 6.0, ((0, 32), (1, 4)), jnp.float32)
    v_velocity = scatter_about(arg_keys[7], (NX, NY), 1.0, 6.0, ((0, 32), (1, 4)), jnp.float32)
    ocean_depth = jnp.clip(jnp.exp(math.log(2.0) - 1.3862944 * jax.random.uniform(arg_keys[8], (NX, NY), jnp.float32) ** level_of(arg_keys[8], (NX, NY), ((0, 32), (1, 4)), -0.2, 0.2)), 0.5, 2.0)
    return {"source_flux": source_flux, "remap_weights": remap_weights, "source_block": source_block, "owner_device": owner_device, "target_row": target_row, "sea_height": sea_height, "u_velocity": u_velocity, "v_velocity": v_velocity, "ocean_depth": ocean_depth}


courant = 0.5
forcing = 0.3
coriolis = 0.2
damping = 0.05
steric = 0.5


def diff_x(field):
    padded = jnp.pad(field, 1)
    return 0.5 * (padded[2:, 1:-1] - padded[:-2, 1:-1])


def diff_y(field):
    padded = jnp.pad(field, 1)
    return 0.5 * (padded[1:-1, 2:] - padded[1:-1, :-2])


def remap_device(packed):
    source_dev, weight_dev, index_dev = packed
    picked = jnp.take(source_dev, index_dev, axis=0).astype(jnp.float32)
    return jnp.einsum('wfb,wbc->wfc', picked, weight_dev.astype(jnp.float32))


def reference(source_flux, remap_weights, source_block, owner_device, target_row, sea_height, u_velocity, v_velocity, ocean_depth):
    device_count = N_ATM * N_OCN
    sources = source_flux.reshape(F, device_count, SB, B).transpose(1, 2, 0, 3)
    weights_dev = remap_weights.reshape(device_count, NW, B, B)
    block_ids = source_block.reshape(device_count, NW)
    contrib = lax.map(remap_device, (sources, weights_dev, block_ids))
    target_ids = (owner_device[:, 0] * CX + target_row).astype(jnp.int32)
    summed = jax.ops.segment_sum(contrib.reshape(-1, F, B), target_ids, num_segments=device_count * CX)
    ocean_flux = summed.reshape(N_ATM, N_OCN, CX, F, B).transpose(3, 0, 2, 1, 4).reshape(F, NX, NY)
    source = forcing * (ocean_flux[2] + steric * ocean_flux[3])
    height = sea_height
    zonal_flow = u_velocity
    merid_flow = v_velocity
    for substep in range(STEPS):
        height = height - courant * ocean_depth * (diff_x(zonal_flow) + diff_y(merid_flow)) + source
        new_zonal = zonal_flow - courant * diff_x(height) + coriolis * merid_flow + forcing * ocean_flux[0] - damping * zonal_flow
        new_merid = merid_flow - courant * diff_y(height) - coriolis * zonal_flow + forcing * ocean_flux[1] - damping * merid_flow
        zonal_flow = new_zonal
        merid_flow = new_merid
    return ocean_flux, height, zonal_flow, merid_flow
```

```python
import functools

import jax
import jax.numpy as jnp
from jax import lax
from jax.experimental import pallas as pl
from jax.experimental.pallas import tpu as pltpu
from jax.sharding import PartitionSpec as P

CX = 64
STEPS = 3
F = 4
B = 128
CAP = 9
ROWS = 40
LABEL_ROW = 39
EDGE = 5
REACH = 6
CHUNKS = 16

courant = 0.5
forcing = 0.3
coriolis = 0.2
damping = 0.05
steric = 0.5

AXES = ("atm", "ocn")


def pack_kernel(
    owner_h,
    target_h,
    block_h,
    src_h,
    weights_h,
    out,
    weights,
    lhs,
    labels,
    src,
    owner,
    target,
    block,
    count,
    sems,
    small_sems,
    *,
    devices,
    ocn,
):
    total = weights.shape[0]
    per = total // CHUNKS
    smalls = [
        pltpu.make_async_copy(a, b, small_sems.at[i])
        for i, (a, b) in enumerate(
            ((src_h, src), (owner_h, owner), (target_h, target), (block_h, block))
        )
    ]
    for copy in smalls:
        copy.start()
    copies = [
        pltpu.make_async_copy(
            weights_h.at[pl.ds(c * per, per)], weights.at[pl.ds(c * per, per)], sems.at[c]
        )
        for c in range(CHUNKS)
    ]
    for copy in copies:
        copy.start()
    out[...] = jnp.zeros(out.shape, jnp.float32)
    labels[...] = jnp.full(labels.shape, -1.0, jnp.float32)

    def clear(i, carry):
        count[i] = 0
        return carry

    lax.fori_loop(0, devices, clear, 0, unroll=8)
    smalls[0].wait()
    zero = jnp.zeros((F, B), jnp.float32)
    for b in range(src.shape[1] // B):
        value = src[:, b * B : (b + 1) * B].astype(jnp.float32)
        for j in range(4):
            parts = [zero] * 4
            parts[j] = value
            lhs[j, b] = jnp.concatenate(parts, 0).astype(jnp.bfloat16)
    for copy in smalls[1:]:
        copy.wait()
    lane = lax.broadcasted_iota(jnp.int32, (1, B), 1)
    for c in range(CHUNKS):
        copies[c].wait()
        for w in range(c * per, (c + 1) * per, 4):
            left = jnp.concatenate([lhs[j, block[w + j]] for j in range(4)], axis=1)
            right = weights[w : w + 4].reshape(4 * B, B)
            rows = jnp.dot(left, right, preferred_element_type=jnp.float32)
            for j in range(4):
                o = owner[w + j]
                k = count[o]
                count[o] = k + 1
                out[pl.ds(o * ROWS + k * F, F), :] = rows[F * j : F * (j + 1)]
                labels[pl.ds(o, 1), :] = jnp.where(
                    lane == k, target[w + j].astype(jnp.float32), labels[pl.ds(o, 1), :]
                )

    lane = lax.broadcasted_iota(jnp.int32, (devices, B), 1)
    edge = [jnp.zeros((devices, B), jnp.float32) for _ in range(4)]
    for k in range(CAP):
        late = k >= 6
        for f in range(F):
            at = (k - 6 if late else k) * F * EDGE + f * EDGE
            here = (lane >= at) & (lane < at + EDGE)
            column = out[pl.ds(k * F + f, devices, stride=ROWS), :]
            last = pltpu.roll(column, (at - (B - EDGE)) % B, 1)
            first = pltpu.roll(column, at, 1) if at else column
            edge[2 * late] = jnp.where(here, last, edge[2 * late])
            edge[2 * late + 1] = jnp.where(here, first, edge[2 * late + 1])
    last, first, last_late, first_late = edge
    out[pl.ds(36, devices, stride=ROWS), :] = pltpu.roll(last, 1, 0)
    late = jnp.where(
        lane < 64,
        pltpu.roll(last_late, 1, 0),
        pltpu.roll(pltpu.roll(first_late, devices - 1, 0), 64, 1),
    )
    out[pl.ds(37, devices, stride=ROWS), :] = late
    out[pl.ds(38, devices, stride=ROWS), :] = pltpu.roll(first, devices - 1, 0)
    place = lax.broadcasted_iota(jnp.int32, (devices, B), 0) % ocn
    own = labels[...]
    before = jnp.where(place > 0, pltpu.roll(pltpu.roll(own, 1, 0), 16, 1), -1.0)
    after = jnp.where(place < ocn - 1, pltpu.roll(pltpu.roll(own, devices - 1, 0), 32, 1), -1.0)
    out[pl.ds(LABEL_ROW, devices, stride=ROWS), :] = jnp.where(
        lane < 16, own, jnp.where(lane < 32, before, jnp.where(lane < 48, after, -1.0))
    )


def pack(owner, target, block, src, weights, devices, ocn):
    total = weights.shape[0]
    here = pl.BlockSpec(memory_space=pltpu.HBM)
    return pl.pallas_call(
        functools.partial(pack_kernel, devices=devices, ocn=ocn),
        out_shape=jax.ShapeDtypeStruct((devices * ROWS, B), jnp.float32),
        in_specs=[here] * 5,
        out_specs=pl.BlockSpec(memory_space=pltpu.VMEM),
        scratch_shapes=[
            pltpu.VMEM(weights.shape, jnp.bfloat16),
            pltpu.VMEM((4, src.shape[1] // B, 4 * F, B), jnp.bfloat16),
            pltpu.VMEM((devices, B), jnp.float32),
            pltpu.VMEM(src.shape, jnp.bfloat16),
            pltpu.SMEM((total,), jnp.int32),
            pltpu.SMEM((total,), jnp.int32),
            pltpu.SMEM((total,), jnp.int32),
            pltpu.SMEM((devices,), jnp.int32),
            pltpu.SemaphoreType.DMA((CHUNKS,)),
            pltpu.SemaphoreType.DMA((4,)),
        ],
        compiler_params=pltpu.CompilerParams(vmem_limit_bytes=48 << 20),
        cost_estimate=pl.CostEstimate(
            flops=2 * F * weights.size, bytes_accessed=2 * weights.size, transcendentals=0
        ),
        name="remap_pack",
    )(owner, target, block, src, weights)


def doubled(value):
    high = value.astype(jnp.bfloat16)
    low = (value - high.astype(jnp.float32)).astype(jnp.bfloat16)
    return jnp.concatenate([high, low], axis=0)


def sum_kernel(arrived, flux, wide, first_rows, last_rows, *, devices):
    names = arrived[pl.ds(LABEL_ROW, devices, stride=ROWS), :].T
    row = lax.broadcasted_iota(jnp.int32, (CX, devices), 0).astype(jnp.float32)

    def pick(lane):
        hot = (row == names[lane : lane + 1, :]).astype(jnp.bfloat16)
        return jnp.concatenate([hot, hot], axis=1)

    total = jnp.zeros((CX, F * B), jnp.float32)
    for k in range(CAP):
        rows = jnp.concatenate(
            [
                doubled(arrived[pl.ds(k * F + f, devices, stride=ROWS), :])
                for f in range(F)
            ],
            axis=1,
        )
        total = total + jnp.dot(pick(k), rows, preferred_element_type=jnp.float32)

    def edges(at, picks):
        rows = doubled(arrived[pl.ds(at, devices, stride=ROWS), :])
        return jnp.dot(jnp.concatenate(picks, 0), rows, preferred_element_type=jnp.float32)

    before = edges(36, [pick(16 + k) for k in range(6)])
    late = edges(37, [pick(16 + k) for k in range(6, 9)] + [pick(32 + k) for k in range(6, 9)])
    after = edges(38, [pick(32 + k) for k in range(6)])

    def shifted(value, k, by):
        return pltpu.roll(value[k * CX : (k + 1) * CX], by % B, 1)

    last = before[:CX]
    first = after[:CX]
    for k in range(1, 6):
        last = last + shifted(before, k, -20 * k)
        first = first + shifted(after, k, -20 * k)
    for k in range(3):
        last = last + shifted(late, k, -20 * k)
        first = first + shifted(late, 3 + k, -64 - 20 * k)
    lane = lax.broadcasted_iota(jnp.int32, (CX, B), 1)
    sides = []
    for f in range(F):
        low = pltpu.roll(last, (B - EDGE - EDGE * f) % B, 1)
        high = pltpu.roll(first, (B - EDGE * f) % B, 1) if f else first
        sides.append(jnp.where(lane >= B - EDGE, low, jnp.where(lane < EDGE, high, 0.0)))
    own = [total[:, f * B : (f + 1) * B] for f in range(F)]
    for f in range(F):
        flux[f] = own[f]
    fields = [
        jnp.concatenate([own[0], sides[0]], axis=1),
        jnp.concatenate([own[1], sides[1]], axis=1),
        jnp.concatenate(
            [
                forcing * (own[2] + steric * own[3]),
                forcing * (sides[2] + steric * sides[3]),
            ],
            axis=1,
        ),
    ]
    for i, field in enumerate(fields):
        wide[i] = field
        first_rows[i] = field[:8]
        last_rows[i] = field[CX - 8 :]


def sum_rows(arrived, devices):
    inside = pl.BlockSpec(memory_space=pltpu.VMEM)
    return pl.pallas_call(
        functools.partial(sum_kernel, devices=devices),
        out_shape=(
            jax.ShapeDtypeStruct((F, CX, B), jnp.float32),
            jax.ShapeDtypeStruct((3, CX, 2 * B), jnp.float32),
            jax.ShapeDtypeStruct((3, 8, 2 * B), jnp.float32),
            jax.ShapeDtypeStruct((3, 8, 2 * B), jnp.float32),
        ),
        in_specs=[inside],
        out_specs=(inside,) * 4,
        compiler_params=pltpu.CompilerParams(vmem_limit_bytes=32 << 20),
        name="sum_rows",
    )(arrived)


def step_kernel(state, wide, above, below, height_out, zonal_out, merid_out):
    rows = CX + 16

    def field(i):
        return jnp.concatenate([above[i], wide[i], below[i]], axis=0)

    zonal_flux, merid_flux, source = field(0), field(1), field(2)
    height, zonal, merid, depth = state[0], state[1], state[2], state[3]
    inside = depth > 0.0

    def grad_x(a):
        return 0.5 * (pltpu.roll(a, rows - 1, 0) - pltpu.roll(a, 1, 0))

    def grad_y(a):
        return 0.5 * (pltpu.roll(a, 2 * B - 1, 1) - pltpu.roll(a, 1, 1))

    for _ in range(STEPS):
        height = height - courant * depth * (grad_x(zonal) + grad_y(merid)) + source
        new_zonal = (
            zonal
            - courant * grad_x(height)
            + coriolis * merid
            + forcing * zonal_flux
            - damping * zonal
        )
        new_merid = (
            merid
            - courant * grad_y(height)
            - coriolis * zonal
            + forcing * merid_flux
            - damping * merid
        )
        zonal = jnp.where(inside, new_zonal, 0.0)
        merid = jnp.where(inside, new_merid, 0.0)
    height_out[...] = height[8 : 8 + CX, :B]
    zonal_out[...] = zonal[8 : 8 + CX, :B]
    merid_out[...] = merid[8 : 8 + CX, :B]


def substeps(state, wide, above, below):
    inside = pl.BlockSpec(memory_space=pltpu.VMEM)
    shape = jax.ShapeDtypeStruct((CX, B), jnp.float32)
    return pl.pallas_call(
        step_kernel,
        out_shape=(shape,) * 3,
        in_specs=[inside] * 4,
        out_specs=(inside,) * 3,
        compiler_params=pltpu.CompilerParams(vmem_limit_bytes=32 << 20),
        name="substeps",
    )(state, wide, above, below)


def from_before(x, axis):
    n = lax.axis_size(axis)
    return lax.ppermute(x, axis, [(i, i + 1) for i in range(n - 1)])


def from_after(x, axis):
    n = lax.axis_size(axis)
    return lax.ppermute(x, axis, [(i + 1, i) for i in range(n - 1)])


def on_device(
    source_flux,
    remap_weights,
    source_block,
    owner_device,
    target_row,
    sea_height,
    u_velocity,
    v_velocity,
    ocean_depth,
):
    ocn = lax.axis_size("ocn")
    devices = lax.axis_size("atm") * ocn
    messages = pack(
        owner_device[:, 0], target_row, source_block, source_flux, remap_weights, devices, ocn
    )
    arrived = lax.all_to_all(messages, AXES, split_axis=0, concat_axis=0, tiled=True)

    state = jnp.stack([sea_height, u_velocity, v_velocity, ocean_depth])
    state, messages = lax.optimization_barrier((state, messages))
    before = from_before(state[:, :, B - REACH :], "ocn")
    after = from_after(state[:, :, :REACH], "ocn")
    gap = jnp.zeros((4, CX, B - 2 * REACH), jnp.float32)
    state = jnp.concatenate([state, after, gap, before], axis=2)
    above = from_before(state[:, CX - 8 :], "atm")
    below = from_after(state[:, :8], "atm")
    state = jnp.concatenate([above, state, below], axis=1)

    flux, wide, first_rows, last_rows = sum_rows(arrived, devices)
    above = from_before(last_rows, "atm")
    below = from_after(first_rows, "atm")
    height, zonal, merid = substeps(state, wide, above, below)
    return flux, height, zonal, merid


def solution(mesh):
    placed = (
        P(None, AXES),
        P(AXES, None, None),
        P(AXES),
        P(AXES, None),
        P(AXES),
        P("atm", "ocn"),
        P("atm", "ocn"),
        P("atm", "ocn"),
        P("atm", "ocn"),
    )
    return jax.shard_map(
        on_device,
        mesh=mesh,
        in_specs=placed,
        out_specs=(P(None, "atm", "ocn"), P("atm", "ocn"), P("atm", "ocn"), P("atm", "ocn")),
        check_vma=False,
    )
```

```python
import functools

import jax
import jax.numpy as jnp
from jax import lax
from jax.experimental import pallas as pl
from jax.experimental.pallas import tpu as pltpu
from jax.sharding import PartitionSpec as P

CX = 64
STEPS = 3
F = 4
B = 128
CAP = 9
ROWS = 38
REACH = 6
SPANS = ((0, 3), (6, 4), (14, 5))
SPAN = 24
SPLIT = 5
LABELS = 96
CHUNKS = 16

courant = 0.5
forcing = 0.3
coriolis = 0.2
damping = 0.05
steric = 0.5

AXES = ("atm", "ocn")


def pack_kernel(
    owner_h,
    target_h,
    block_h,
    src_h,
    weights_h,
    out,
    weights,
    lhs,
    labels,
    src,
    owner,
    target,
    block,
    count,
    built,
    sems,
    small_sems,
    out_sems,
    *,
    devices,
    ocn,
):
    total = weights.shape[0]
    per = total // CHUNKS
    smalls = [
        pltpu.make_async_copy(a, b, small_sems.at[i])
        for i, (a, b) in enumerate(
            ((src_h, src), (owner_h, owner), (target_h, target), (block_h, block))
        )
    ]
    for copy in smalls:
        copy.start()
    copies = [
        pltpu.make_async_copy(
            weights_h.at[pl.ds(c * per, per)], weights.at[pl.ds(c * per, per)], sems.at[c]
        )
        for c in range(CHUNKS)
    ]
    copies[0].start()
    built[...] = jnp.zeros(built.shape, jnp.float32)
    labels[...] = jnp.full(labels.shape, -1.0, jnp.float32)

    def clear(i, carry):
        count[i] = 0
        return carry

    lax.fori_loop(0, devices, clear, 0, unroll=8)
    smalls[0].wait()
    zero = jnp.zeros((F, B), jnp.float32)
    for b in range(src.shape[1] // B):
        value = src[:, b * B : (b + 1) * B].astype(jnp.float32)
        for j in range(4):
            parts = [zero] * 4
            parts[j] = value
            lhs[j, b] = jnp.concatenate(parts, 0).astype(jnp.bfloat16)
    for copy in smalls[1:]:
        copy.wait()
    for copy in copies[1:]:
        copy.start()
    lane = lax.broadcasted_iota(jnp.int32, (1, B), 1)
    for c in range(CHUNKS):
        copies[c].wait()
        for w in range(c * per, (c + 1) * per, 4):
            left = jnp.concatenate([lhs[j, block[w + j]] for j in range(4)], axis=1)
            right = weights[w : w + 4].reshape(4 * B, B)
            rows = jnp.dot(left, right, preferred_element_type=jnp.float32)
            for j in range(4):
                o = owner[w + j]
                k = count[o]
                count[o] = k + 1
                built[pl.ds(o * ROWS + k * F, F), :] = rows[F * j : F * (j + 1)]
                labels[pl.ds(o, 1), :] = jnp.where(
                    lane == k, target[w + j].astype(jnp.float32), labels[pl.ds(o, 1), :]
                )

    group = 8 * ocn
    lane = lax.broadcasted_iota(jnp.int32, (group, B), 1)
    place = lax.broadcasted_iota(jnp.int32, (group, B), 0) % ocn
    sends = []
    for g in range(devices // group):
        base = g * group * ROWS
        edge = [jnp.zeros((group, B), jnp.float32) for _ in range(2)]
        from_before = [lane < 0, lane < 0]
        for k in range(CAP):
            part = k // SPLIT
            rows = [built[pl.ds(base + k * F + f, group, stride=ROWS), :] for f in range(F)]
            rows = [rows[0], rows[1], forcing * (rows[2] + steric * rows[3])]
            for (start, width), value in zip(SPANS, rows):
                at = (k % SPLIT) * SPAN + start
                moved = pltpu.roll(value, (at - (B - width)) % B, 1)
                edge[part] = jnp.where((lane >= at) & (lane < at + 2 * width), moved, edge[part])
                from_before[part] |= (lane >= at) & (lane < at + width)
        sides = [
            jnp.where(mask, pltpu.roll(value, 1, 0), pltpu.roll(value, group - 1, 0))
            for mask, value in zip(from_before, edge)
        ]
        own = labels[pl.ds(g * group, group), :]
        before = jnp.where(place > 0, pltpu.roll(own, 1, 0), -1.0)
        after = jnp.where(place < ocn - 1, pltpu.roll(own, group - 1, 0), -1.0)
        for i, names in enumerate((own, before, after)):
            at = LABELS + CAP * i
            sides[1] = jnp.where(
                (lane >= at) & (lane < at + CAP), pltpu.roll(names, at, 1), sides[1]
            )
        built[pl.ds(base + 36, group, stride=ROWS), :] = sides[0]
        built[pl.ds(base + 37, group, stride=ROWS), :] = sides[1]
        span = pl.ds(base, group * ROWS)
        send = pltpu.make_async_copy(built.at[span], out.at[span], out_sems.at[g])
        send.start()
        sends.append(send)
    for send in sends:
        send.wait()


def pack(owner, target, block, src, weights, devices, ocn):
    total = weights.shape[0]
    here = pl.BlockSpec(memory_space=pltpu.HBM)
    return pl.pallas_call(
        functools.partial(pack_kernel, devices=devices, ocn=ocn),
        out_shape=jax.ShapeDtypeStruct((devices * ROWS, B), jnp.float32),
        in_specs=[here] * 5,
        out_specs=here,
        scratch_shapes=[
            pltpu.VMEM(weights.shape, jnp.bfloat16),
            pltpu.VMEM((4, src.shape[1] // B, 4 * F, B), jnp.bfloat16),
            pltpu.VMEM((devices, B), jnp.float32),
            pltpu.VMEM(src.shape, jnp.bfloat16),
            pltpu.SMEM((total,), jnp.int32),
            pltpu.SMEM((total,), jnp.int32),
            pltpu.SMEM((total,), jnp.int32),
            pltpu.SMEM((devices,), jnp.int32),
            pltpu.VMEM((devices * ROWS, B), jnp.float32),
            pltpu.SemaphoreType.DMA((CHUNKS,)),
            pltpu.SemaphoreType.DMA((4,)),
            pltpu.SemaphoreType.DMA((devices // (8 * ocn),)),
        ],
        compiler_params=pltpu.CompilerParams(vmem_limit_bytes=60 << 20),
        cost_estimate=pl.CostEstimate(
            flops=2 * F * weights.size, bytes_accessed=2 * weights.size, transcendentals=0
        ),
        name="remap_pack",
    )(owner, target, block, src, weights)


def doubled(value):
    high = value.astype(jnp.bfloat16)
    low = (value - high.astype(jnp.float32)).astype(jnp.bfloat16)
    return jnp.concatenate([high, low], axis=0)


def sum_kernel(parity, arrived, state, flux, wide, to_pair, to_beside, *, devices):
    names = arrived[pl.ds(37, devices, stride=ROWS), :].T
    row = lax.broadcasted_iota(jnp.int32, (CX, devices), 0).astype(jnp.float32)

    def pick(lane):
        hot = (row == names[lane : lane + 1, :]).astype(jnp.bfloat16)
        return jnp.concatenate([hot, hot], axis=1)

    total = jnp.zeros((CX, F * B), jnp.float32)
    for k in range(CAP):
        rows = jnp.concatenate(
            [
                doubled(arrived[pl.ds(k * F + f, devices, stride=ROWS), :])
                for f in range(F)
            ],
            axis=1,
        )
        total = total + jnp.dot(pick(LABELS + k), rows, preferred_element_type=jnp.float32)

    rows = jnp.concatenate(
        [doubled(arrived[pl.ds(at, devices, stride=ROWS), :]) for at in (36, 37)], axis=0
    )
    none = jnp.zeros((CX, 2 * devices), jnp.bfloat16)
    sums = []
    for side in (LABELS + CAP, LABELS + 2 * CAP):
        hot = jnp.concatenate(
            [
                jnp.concatenate(
                    [pick(side + k), pick(side + SPLIT + k) if SPLIT + k < CAP else none], axis=1
                )
                for k in range(SPLIT)
            ],
            axis=0,
        )
        found = jnp.dot(hot, rows, preferred_element_type=jnp.float32)
        value = found[:CX]
        for k in range(1, SPLIT):
            value = value + pltpu.roll(found[k * CX : (k + 1) * CX], B - SPAN * k, 1)
        sums.append(value)
    lane = lax.broadcasted_iota(jnp.int32, (CX, B), 1)
    from_before = lane < 0
    for start, width in SPANS:
        from_before |= (lane >= start) & (lane < start + width)
    beside = jnp.where(from_before, sums[0], sums[1])
    own = [total[:, f * B : (f + 1) * B] for f in range(F)]
    for f in range(F):
        flux[f] = own[f]
    own = [own[0], own[1], forcing * (own[2] + steric * own[3])]
    fields = []
    for (start, width), value in zip(SPANS, own):
        moved = pltpu.roll(beside, B - width - start, 1)
        outer = jnp.where((lane >= B - width) | (lane < width), moved, 0.0)
        fields.append(jnp.concatenate([value, outer], axis=1))
    for i, field in enumerate(fields):
        wide[i] = field
    odd = parity[0] == 1
    firsts = [field[:8] for field in fields] + [state[i, :8] for i in range(4)]
    lasts = [field[CX - 8 :] for field in fields] + [state[i, CX - 8 :] for i in range(4)]
    for i, (first, last) in enumerate(zip(firsts, lasts)):
        to_pair[i] = jnp.where(odd, first, last)
        to_beside[i] = jnp.where(odd, last, first)


def sum_rows(parity, arrived, state, devices):
    inside = pl.BlockSpec(memory_space=pltpu.VMEM)
    return pl.pallas_call(
        functools.partial(sum_kernel, devices=devices),
        out_shape=(
            jax.ShapeDtypeStruct((F, CX, B), jnp.float32),
            jax.ShapeDtypeStruct((3, CX, 2 * B), jnp.float32),
            jax.ShapeDtypeStruct((7, 8, 2 * B), jnp.float32),
            jax.ShapeDtypeStruct((7, 8, 2 * B), jnp.float32),
        ),
        in_specs=[pl.BlockSpec(memory_space=pltpu.SMEM), inside, inside],
        out_specs=(inside,) * 4,
        compiler_params=pltpu.CompilerParams(vmem_limit_bytes=32 << 20),
        name="sum_rows",
    )(parity, arrived, state)


def step_kernel(place, state, wide, pair, beside, height_out, zonal_out, merid_out):
    rows = CX + 16
    odd = place[0] == 1
    has_above = place[1] == 1
    has_below = place[2] == 1

    def field(i):
        above = jnp.where(odd, pair[i], beside[i])
        below = jnp.where(odd, beside[i], pair[i])
        own = wide[i] if i < 3 else state[i - 3]
        return jnp.concatenate(
            [jnp.where(has_above, above, 0.0), own, jnp.where(has_below, below, 0.0)], axis=0
        )

    zonal_flux, merid_flux, source = field(0), field(1), field(2)
    height, zonal, merid, depth = field(3), field(4), field(5), field(6)
    inside = depth > 0.0

    def grad_x(a):
        return 0.5 * (pltpu.roll(a, rows - 1, 0) - pltpu.roll(a, 1, 0))

    def grad_y(a):
        return 0.5 * (pltpu.roll(a, 2 * B - 1, 1) - pltpu.roll(a, 1, 1))

    for _ in range(STEPS):
        height = height - courant * depth * (grad_x(zonal) + grad_y(merid)) + source
        new_zonal = (
            zonal
            - courant * grad_x(height)
            + coriolis * merid
            + forcing * zonal_flux
            - damping * zonal
        )
        new_merid = (
            merid
            - courant * grad_y(height)
            - coriolis * zonal
            + forcing * merid_flux
            - damping * merid
        )
        zonal = jnp.where(inside, new_zonal, 0.0)
        merid = jnp.where(inside, new_merid, 0.0)
    height_out[...] = height[8 : 8 + CX, :B]
    zonal_out[...] = zonal[8 : 8 + CX, :B]
    merid_out[...] = merid[8 : 8 + CX, :B]


def substeps(place, state, wide, pair, beside):
    inside = pl.BlockSpec(memory_space=pltpu.VMEM)
    shape = jax.ShapeDtypeStruct((CX, B), jnp.float32)
    return pl.pallas_call(
        step_kernel,
        out_shape=(shape,) * 3,
        in_specs=[pl.BlockSpec(memory_space=pltpu.SMEM)] + [inside] * 4,
        out_specs=(inside,) * 3,
        compiler_params=pltpu.CompilerParams(vmem_limit_bytes=32 << 20),
        name="substeps",
    )(place, state, wide, pair, beside)


def around(x, axis, by):
    n = lax.axis_size(axis)
    return lax.ppermute(x, axis, [(i, (i + by) % n) for i in range(n)])


def on_device(
    source_flux,
    remap_weights,
    source_block,
    owner_device,
    target_row,
    sea_height,
    u_velocity,
    v_velocity,
    ocean_depth,
):
    ocn = lax.axis_size("ocn")
    devices = lax.axis_size("atm") * ocn
    messages = pack(
        owner_device[:, 0], target_row, source_block, source_flux, remap_weights, devices, ocn
    )
    arrived = lax.all_to_all(
        messages.reshape(-1, 1, B), AXES, split_axis=0, concat_axis=0, tiled=True
    ).reshape(-1, B)

    column = lax.axis_index("ocn")
    line = lax.axis_index("atm")
    lines = lax.axis_size("atm")
    place = jnp.stack([line % 2, line > 0, line < lines - 1]).astype(jnp.int32)
    state = jnp.stack([sea_height, u_velocity, v_velocity, ocean_depth])
    state, messages = lax.optimization_barrier((state, messages))
    before = around(state[:, :, B - REACH :], "ocn", 1)
    after = around(state[:, :, :REACH], "ocn", -1)
    before = jnp.where(column > 0, before, 0.0)
    after = jnp.where(column < ocn - 1, after, 0.0)
    gap = jnp.zeros((4, CX, B - 2 * REACH), jnp.float32)
    state = jnp.concatenate([state, after, gap, before], axis=2)

    flux, wide, to_pair, to_beside = sum_rows(place[:1], arrived, state, devices)
    pair = lax.ppermute(to_pair, "atm", [(i, i ^ 1) for i in range(lines)])
    beside = lax.ppermute(
        to_beside, "atm", [(i, (i + 1 if i % 2 else i - 1) % lines) for i in range(lines)]
    )
    height, zonal, merid = substeps(place, state, wide, pair, beside)
    return flux, height, zonal, merid


def solution(mesh):
    placed = (
        P(None, AXES),
        P(AXES, None, None),
        P(AXES),
        P(AXES, None),
        P(AXES),
        P("atm", "ocn"),
        P("atm", "ocn"),
        P("atm", "ocn"),
        P("atm", "ocn"),
    )
    return jax.shard_map(
        on_device,
        mesh=mesh,
        in_specs=placed,
        out_specs=(P(None, "atm", "ocn"), P("atm", "ocn"), P("atm", "ocn"), P("atm", "ocn")),
        check_vma=False,
    )
```

```python
import functools

import jax
import jax.numpy as jnp
from jax import lax
from jax.experimental import pallas as pl
from jax.experimental.pallas import tpu as pltpu
from jax.sharding import PartitionSpec as P

CX = 64
STEPS = 3
F = 4
B = 128
CAP = 9
ROWS = 38
REACH = 6
SPANS = ((0, 3), (6, 4), (14, 5))
SPAN = 24
SPLIT = 5
LABELS = 96
CHUNKS = 16
AHEAD = 2

courant = 0.5
forcing = 0.3
coriolis = 0.2
damping = 0.05
steric = 0.5

AXES = ("atm", "ocn")


def pack_kernel(
    owner_h,
    target_h,
    block_h,
    src_h,
    weights_h,
    out,
    weights,
    lhs,
    labels,
    src,
    owner,
    target,
    block,
    count,
    built,
    sems,
    small_sems,
    out_sems,
    *,
    devices,
    ocn,
):
    total = weights.shape[0]
    per = total // CHUNKS
    smalls = [
        pltpu.make_async_copy(a, b, small_sems.at[i])
        for i, (a, b) in enumerate(
            ((src_h, src), (owner_h, owner), (target_h, target), (block_h, block))
        )
    ]
    for copy in smalls:
        copy.start()
    copies = [
        pltpu.make_async_copy(
            weights_h.at[pl.ds(c * per, per)], weights.at[pl.ds(c * per, per)], sems.at[c]
        )
        for c in range(CHUNKS)
    ]
    for copy in copies[:AHEAD]:
        copy.start()
    built[...] = jnp.zeros(built.shape, jnp.float32)
    labels[...] = jnp.full(labels.shape, -1.0, jnp.float32)

    def clear(i, carry):
        count[i] = 0
        return carry

    lax.fori_loop(0, devices, clear, 0, unroll=8)
    smalls[0].wait()
    zero = jnp.zeros((F, B), jnp.float32)
    for b in range(src.shape[1] // B):
        value = src[:, b * B : (b + 1) * B].astype(jnp.float32)
        for j in range(4):
            parts = [zero] * 4
            parts[j] = value
            lhs[j, b] = jnp.concatenate(parts, 0).astype(jnp.bfloat16)
    for copy in smalls[1:]:
        copy.wait()
    for copy in copies[AHEAD:]:
        copy.start()
    lane = lax.broadcasted_iota(jnp.int32, (1, B), 1)
    for c in range(CHUNKS):
        copies[c].wait()
        for w in range(c * per, (c + 1) * per, 4):
            left = jnp.concatenate([lhs[j, block[w + j]] for j in range(4)], axis=1)
            right = weights[w : w + 4].reshape(4 * B, B)
            rows = jnp.dot(left, right, preferred_element_type=jnp.float32)
            for j in range(4):
                o = owner[0, w + j]
                k = count[o]
                count[o] = k + 1
                built[pl.ds(o * ROWS + k * F, F), :] = rows[F * j : F * (j + 1)]
                labels[pl.ds(o, 1), :] = jnp.where(
                    lane == k, target[w + j].astype(jnp.float32), labels[pl.ds(o, 1), :]
                )

    group = 8 * ocn
    lane = lax.broadcasted_iota(jnp.int32, (group, B), 1)
    place = lax.broadcasted_iota(jnp.int32, (group, B), 0) % ocn
    sends = []
    for g in range(devices // group):
        base = g * group * ROWS
        edge = [jnp.zeros((group, B), jnp.float32) for _ in range(2)]
        from_before = [lane < 0, lane < 0]
        for k in range(CAP):
            part = k // SPLIT
            rows = [built[pl.ds(base + k * F + f, group, stride=ROWS), :] for f in range(F)]
            rows = [rows[0], rows[1], forcing * (rows[2] + steric * rows[3])]
            for (start, width), value in zip(SPANS, rows):
                at = (k % SPLIT) * SPAN + start
                moved = pltpu.roll(value, (at - (B - width)) % B, 1)
                edge[part] = jnp.where((lane >= at) & (lane < at + 2 * width), moved, edge[part])
                from_before[part] |= (lane >= at) & (lane < at + width)
        sides = [
            jnp.where(mask, pltpu.roll(value, 1, 0), pltpu.roll(value, group - 1, 0))
            for mask, value in zip(from_before, edge)
        ]
        own = labels[pl.ds(g * group, group), :]
        before = jnp.where(place > 0, pltpu.roll(own, 1, 0), -1.0)
        after = jnp.where(place < ocn - 1, pltpu.roll(own, group - 1, 0), -1.0)
        for i, names in enumerate((own, before, after)):
            at = LABELS + CAP * i
            sides[1] = jnp.where(
                (lane >= at) & (lane < at + CAP), pltpu.roll(names, at, 1), sides[1]
            )
        built[pl.ds(base + 36, group, stride=ROWS), :] = sides[0]
        built[pl.ds(base + 37, group, stride=ROWS), :] = sides[1]
        span = pl.ds(base, group * ROWS)
        send = pltpu.make_async_copy(built.at[span], out.at[span], out_sems.at[g])
        send.start()
        sends.append(send)
    for send in sends:
        send.wait()


def pack(owner, target, block, src, weights, devices, ocn):
    total = weights.shape[0]
    here = pl.BlockSpec(memory_space=pltpu.HBM)
    return pl.pallas_call(
        functools.partial(pack_kernel, devices=devices, ocn=ocn),
        out_shape=jax.ShapeDtypeStruct((devices * ROWS, B), jnp.float32),
        in_specs=[here] * 5,
        out_specs=here,
        scratch_shapes=[
            pltpu.VMEM(weights.shape, jnp.bfloat16),
            pltpu.VMEM((4, src.shape[1] // B, 4 * F, B), jnp.bfloat16),
            pltpu.VMEM((devices, B), jnp.float32),
            pltpu.VMEM(src.shape, jnp.bfloat16),
            pltpu.SMEM((1, total), jnp.int32),
            pltpu.SMEM((total,), jnp.int32),
            pltpu.SMEM((total,), jnp.int32),
            pltpu.SMEM((devices,), jnp.int32),
            pltpu.VMEM((devices * ROWS, B), jnp.float32),
            pltpu.SemaphoreType.DMA((CHUNKS,)),
            pltpu.SemaphoreType.DMA((4,)),
            pltpu.SemaphoreType.DMA((devices // (8 * ocn),)),
        ],
        compiler_params=pltpu.CompilerParams(vmem_limit_bytes=60 << 20),
        cost_estimate=pl.CostEstimate(
            flops=2 * F * weights.size, bytes_accessed=2 * weights.size, transcendentals=0
        ),
        name="remap_pack",
    )(owner, target, block, src, weights)


def doubled(value):
    high = value.astype(jnp.bfloat16)
    low = (value - high.astype(jnp.float32)).astype(jnp.bfloat16)
    return jnp.concatenate([high, low], axis=0)


def sum_kernel(arrived, state, flux, wide, to_pair, to_beside, *, devices):
    names = arrived[pl.ds(37, devices, stride=ROWS), :].T
    row = lax.broadcasted_iota(jnp.int32, (CX, devices), 0).astype(jnp.float32)

    def pick(lane):
        hot = (row == names[lane : lane + 1, :]).astype(jnp.bfloat16)
        return jnp.concatenate([hot, hot], axis=1)

    total = jnp.zeros((CX, F * B), jnp.float32)
    for k in range(CAP):
        rows = jnp.concatenate(
            [
                doubled(arrived[pl.ds(k * F + f, devices, stride=ROWS), :])
                for f in range(F)
            ],
            axis=1,
        )
        total = total + jnp.dot(pick(LABELS + k), rows, preferred_element_type=jnp.float32)

    rows = jnp.concatenate(
        [doubled(arrived[pl.ds(at, devices, stride=ROWS), :]) for at in (36, 37)], axis=0
    )
    none = jnp.zeros((CX, 2 * devices), jnp.bfloat16)
    sums = []
    for side in (LABELS + CAP, LABELS + 2 * CAP):
        hot = jnp.concatenate(
            [
                jnp.concatenate(
                    [pick(side + k), pick(side + SPLIT + k) if SPLIT + k < CAP else none], axis=1
                )
                for k in range(SPLIT)
            ],
            axis=0,
        )
        found = jnp.dot(hot, rows, preferred_element_type=jnp.float32)
        value = found[:CX]
        for k in range(1, SPLIT):
            value = value + pltpu.roll(found[k * CX : (k + 1) * CX], B - SPAN * k, 1)
        sums.append(value)
    lane = lax.broadcasted_iota(jnp.int32, (CX, B), 1)
    from_before = lane < 0
    for start, width in SPANS:
        from_before |= (lane >= start) & (lane < start + width)
    beside = jnp.where(from_before, sums[0], sums[1])
    own = [total[:, f * B : (f + 1) * B] for f in range(F)]
    for f in range(F):
        flux[f] = own[f]
    own = [own[0], own[1], forcing * (own[2] + steric * own[3])]
    fields = []
    for (start, width), value in zip(SPANS, own):
        moved = pltpu.roll(beside, B - width - start, 1)
        outer = jnp.where((lane >= B - width) | (lane < width), moved, 0.0)
        fields.append(jnp.concatenate([value, outer], axis=1))
    for i, field in enumerate(fields):
        wide[i] = field
    odd = lax.axis_index("atm") % 2 == 1
    firsts = [field[:8] for field in fields] + [state[i, :8] for i in range(4)]
    lasts = [field[CX - 8 :] for field in fields] + [state[i, CX - 8 :] for i in range(4)]
    for i, (first, last) in enumerate(zip(firsts, lasts)):
        to_pair[i] = jnp.where(odd, first, last)
        to_beside[i] = jnp.where(odd, last, first)


def sum_rows(arrived, state, devices):
    inside = pl.BlockSpec(memory_space=pltpu.VMEM)
    return pl.pallas_call(
        functools.partial(sum_kernel, devices=devices),
        out_shape=(
            jax.ShapeDtypeStruct((F, CX, B), jnp.float32),
            jax.ShapeDtypeStruct((3, CX, 2 * B), jnp.float32),
            jax.ShapeDtypeStruct((7, 8, 2 * B), jnp.float32),
            jax.ShapeDtypeStruct((7, 8, 2 * B), jnp.float32),
        ),
        in_specs=[inside] * 2,
        out_specs=(inside,) * 4,
        compiler_params=pltpu.CompilerParams(vmem_limit_bytes=32 << 20),
        name="sum_rows",
    )(arrived, state)


def step_kernel(
    state, flux, wide, pair, beside, flux_out, height_out, zonal_out, merid_out, sem, *, lines
):
    send = pltpu.make_async_copy(flux, flux_out, sem)
    send.start()
    rows = CX + 16
    line = lax.axis_index("atm")
    odd = line % 2 == 1
    has_above = line > 0
    has_below = line < lines - 1

    def field(i):
        above = jnp.where(odd, pair[i], beside[i])
        below = jnp.where(odd, beside[i], pair[i])
        own = wide[i] if i < 3 else state[i - 3]
        return jnp.concatenate(
            [jnp.where(has_above, above, 0.0), own, jnp.where(has_below, below, 0.0)], axis=0
        )

    zonal_flux, merid_flux, source = field(0), field(1), field(2)
    height, zonal, merid, depth = field(3), field(4), field(5), field(6)
    inside = depth > 0.0

    def grad_x(a):
        return 0.5 * (pltpu.roll(a, rows - 1, 0) - pltpu.roll(a, 1, 0))

    def grad_y(a):
        return 0.5 * (pltpu.roll(a, 2 * B - 1, 1) - pltpu.roll(a, 1, 1))

    for _ in range(STEPS):
        height = height - courant * depth * (grad_x(zonal) + grad_y(merid)) + source
        new_zonal = (
            zonal
            - courant * grad_x(height)
            + coriolis * merid
            + forcing * zonal_flux
            - damping * zonal
        )
        new_merid = (
            merid
            - courant * grad_y(height)
            - coriolis * zonal
            + forcing * merid_flux
            - damping * merid
        )
        zonal = jnp.where(inside, new_zonal, 0.0)
        merid = jnp.where(inside, new_merid, 0.0)
    height_out[...] = height[8 : 8 + CX, :B]
    zonal_out[...] = zonal[8 : 8 + CX, :B]
    merid_out[...] = merid[8 : 8 + CX, :B]
    send.wait()


def substeps(state, flux, wide, pair, beside, lines):
    inside = pl.BlockSpec(memory_space=pltpu.VMEM)
    shape = jax.ShapeDtypeStruct((CX, B), jnp.float32)
    return pl.pallas_call(
        functools.partial(step_kernel, lines=lines),
        out_shape=(jax.ShapeDtypeStruct((F, CX, B), jnp.float32),) + (shape,) * 3,
        in_specs=[inside] * 5,
        out_specs=(pl.BlockSpec(memory_space=pltpu.HBM),) + (inside,) * 3,
        scratch_shapes=[pltpu.SemaphoreType.DMA],
        compiler_params=pltpu.CompilerParams(vmem_limit_bytes=32 << 20),
        name="substeps",
    )(state, flux, wide, pair, beside)


def around(x, axis, by):
    n = lax.axis_size(axis)
    return lax.ppermute(x, axis, [(i, (i + by) % n) for i in range(n)])


def on_device(
    source_flux,
    remap_weights,
    source_block,
    owner_device,
    target_row,
    sea_height,
    u_velocity,
    v_velocity,
    ocean_depth,
):
    ocn = lax.axis_size("ocn")
    devices = lax.axis_size("atm") * ocn
    messages = pack(
        owner_device.T, target_row, source_block, source_flux, remap_weights, devices, ocn
    )
    arrived = lax.all_to_all(
        messages.reshape(-1, 1, B), AXES, split_axis=0, concat_axis=0, tiled=True
    ).reshape(-1, B)

    column = lax.axis_index("ocn")
    lines = lax.axis_size("atm")
    state = jnp.stack([sea_height, u_velocity, v_velocity, ocean_depth])
    state, messages = lax.optimization_barrier((state, messages))
    before = around(state[:, :, B - REACH :], "ocn", 1)
    after = around(state[:, :, :REACH], "ocn", -1)
    before = jnp.where(column > 0, before, 0.0)
    after = jnp.where(column < ocn - 1, after, 0.0)
    gap = jnp.zeros((4, CX, B - 2 * REACH), jnp.float32)
    state = jnp.concatenate([state, after, gap, before], axis=2)

    flux, wide, to_pair, to_beside = sum_rows(arrived, state, devices)
    pair = lax.ppermute(to_pair, "atm", [(i, i ^ 1) for i in range(lines)])
    beside = lax.ppermute(
        to_beside, "atm", [(i, (i + 1 if i % 2 else i - 1) % lines) for i in range(lines)]
    )
    return substeps(state, flux, wide, pair, beside, lines)


def solution(mesh):
    placed = (
        P(None, AXES),
        P(AXES, None, None),
        P(AXES),
        P(AXES, None),
        P(AXES),
        P("atm", "ocn"),
        P("atm", "ocn"),
        P("atm", "ocn"),
        P("atm", "ocn"),
    )
    return jax.shard_map(
        on_device,
        mesh=mesh,
        in_specs=placed,
        out_specs=(P(None, "atm", "ocn"), P("atm", "ocn"), P("atm", "ocn"), P("atm", "ocn")),
        check_vma=False,
    )
```

```python
import functools

import jax
import jax.numpy as jnp
from jax import lax
from jax.experimental import pallas as pl
from jax.experimental.pallas import tpu as pltpu
from jax.sharding import PartitionSpec as P

CX = 64
STEPS = 3
F = 4
B = 128
CAP = 9
ROWS = 38
REACH = 6
SPANS = ((0, 3), (6, 4), (14, 5))
SPAN = 24
SPLIT = 5
LABELS = 96
CHUNKS = 24
GROUP = 4

courant = 0.5
forcing = 0.3
coriolis = 0.2
damping = 0.05
steric = 0.5

AXES = ("atm", "ocn")


def pack_kernel(
    owner_h,
    target_h,
    block_h,
    src_h,
    weights_h,
    out,
    weights,
    lhs,
    labels,
    src,
    owner,
    target,
    block,
    count,
    built,
    sems,
    small_sems,
    out_sems,
    *,
    devices,
    ocn,
):
    total = weights.shape[0]
    per = total // CHUNKS
    smalls = [
        pltpu.make_async_copy(a, b, small_sems.at[i])
        for i, (a, b) in enumerate(
            ((src_h, src), (owner_h, owner), (target_h, target), (block_h, block))
        )
    ]
    for copy in smalls:
        copy.start(priority=0)
    copies = [
        pltpu.make_async_copy(
            weights_h.at[pl.ds(c * per, per)], weights.at[pl.ds(c * per, per)], sems.at[c]
        )
        for c in range(CHUNKS)
    ]
    for copy in copies:
        copy.start(priority=1)
    built[...] = jnp.zeros(built.shape, jnp.float32)
    labels[...] = jnp.full(labels.shape, -1.0, jnp.float32)

    def clear(i, carry):
        count[i] = 0
        return carry

    lax.fori_loop(0, devices, clear, 0, unroll=8)
    smalls[0].wait()
    zero = jnp.zeros((F, B), jnp.float32)
    for b in range(src.shape[1] // B):
        value = src[:, b * B : (b + 1) * B].astype(jnp.float32)
        for j in range(4):
            parts = [zero] * 4
            parts[j] = value
            lhs[j, b] = jnp.concatenate(parts, 0).astype(jnp.bfloat16)
    for copy in smalls[1:]:
        copy.wait()
    lane = lax.broadcasted_iota(jnp.int32, (1, B), 1)
    for c in range(CHUNKS):
        copies[c].wait()
        for w in range(c * per, (c + 1) * per, 4):
            left = jnp.concatenate([lhs[j, block[w + j]] for j in range(4)], axis=1)
            right = weights[w : w + 4].reshape(4 * B, B)
            rows = jnp.dot(left, right, preferred_element_type=jnp.float32)
            for j in range(4):
                o = owner[0, w + j]
                k = count[o]
                count[o] = k + 1
                built[pl.ds(o * ROWS + k * F, F), :] = rows[F * j : F * (j + 1)]
                name = jnp.full((1, B), target[w + j].astype(jnp.float32))
                pltpu.store(labels.at[pl.ds(o, 1), :], name, mask=lane == k)

    group = GROUP * ocn
    lane = lax.broadcasted_iota(jnp.int32, (group, B), 1)
    place = lax.broadcasted_iota(jnp.int32, (group, B), 0) % ocn
    sends = []
    for g in range(devices // group):
        base = g * group * ROWS
        edge = [jnp.zeros((group, B), jnp.float32) for _ in range(2)]
        from_before = [lane < 0, lane < 0]
        for k in range(CAP):
            part = k // SPLIT
            rows = [built[pl.ds(base + k * F + f, group, stride=ROWS), :] for f in range(F)]
            rows = [rows[0], rows[1], forcing * (rows[2] + steric * rows[3])]
            for (start, width), value in zip(SPANS, rows):
                at = (k % SPLIT) * SPAN + start
                moved = pltpu.roll(value, (at - (B - width)) % B, 1)
                edge[part] = jnp.where((lane >= at) & (lane < at + 2 * width), moved, edge[part])
                from_before[part] |= (lane >= at) & (lane < at + width)
        sides = [
            jnp.where(mask, pltpu.roll(value, 1, 0), pltpu.roll(value, group - 1, 0))
            for mask, value in zip(from_before, edge)
        ]
        own = labels[pl.ds(g * group, group), :]
        before = jnp.where(place > 0, pltpu.roll(own, 1, 0), -1.0)
        after = jnp.where(place < ocn - 1, pltpu.roll(own, group - 1, 0), -1.0)
        for i, names in enumerate((own, before, after)):
            at = LABELS + CAP * i
            sides[1] = jnp.where(
                (lane >= at) & (lane < at + CAP), pltpu.roll(names, at, 1), sides[1]
            )
        built[pl.ds(base + 36, group, stride=ROWS), :] = sides[0]
        built[pl.ds(base + 37, group, stride=ROWS), :] = sides[1]
        span = pl.ds(base, group * ROWS)
        send = pltpu.make_async_copy(built.at[span], out.at[span], out_sems.at[g])
        send.start()
        sends.append(send)
    for send in sends:
        send.wait()


def pack(owner, target, block, src, weights, devices, ocn):
    total = weights.shape[0]
    here = pl.BlockSpec(memory_space=pltpu.HBM)
    return pl.pallas_call(
        functools.partial(pack_kernel, devices=devices, ocn=ocn),
        out_shape=jax.ShapeDtypeStruct((devices * ROWS, B), jnp.float32),
        in_specs=[here] * 5,
        out_specs=here,
        scratch_shapes=[
            pltpu.VMEM(weights.shape, jnp.bfloat16),
            pltpu.VMEM((4, src.shape[1] // B, 4 * F, B), jnp.bfloat16),
            pltpu.VMEM((devices, B), jnp.float32),
            pltpu.VMEM(src.shape, jnp.bfloat16),
            pltpu.SMEM((1, total), jnp.int32),
            pltpu.SMEM((total,), jnp.int32),
            pltpu.SMEM((total,), jnp.int32),
            pltpu.SMEM((devices,), jnp.int32),
            pltpu.VMEM((devices * ROWS, B), jnp.float32),
            pltpu.SemaphoreType.DMA((CHUNKS,)),
            pltpu.SemaphoreType.DMA((4,)),
            pltpu.SemaphoreType.DMA((devices // (GROUP * ocn),)),
        ],
        compiler_params=pltpu.CompilerParams(vmem_limit_bytes=60 << 20),
        cost_estimate=pl.CostEstimate(
            flops=2 * F * weights.size, bytes_accessed=2 * weights.size, transcendentals=0
        ),
        name="remap_pack",
    )(owner, target, block, src, weights)


def doubled(value):
    high = value.astype(jnp.bfloat16)
    low = (value - high.astype(jnp.float32)).astype(jnp.bfloat16)
    return jnp.concatenate([high, low], axis=0)


def sum_kernel(arrived, state, flux, wide, to_pair, to_beside, *, devices):
    names = arrived[pl.ds(37, devices, stride=ROWS), :].T
    row = lax.broadcasted_iota(jnp.int32, (CX, devices), 0).astype(jnp.float32)

    def pick(lane):
        hot = (row == names[lane : lane + 1, :]).astype(jnp.bfloat16)
        return jnp.concatenate([hot, hot], axis=1)

    total = jnp.zeros((CX, F * B), jnp.float32)
    for k in range(CAP):
        rows = jnp.concatenate(
            [
                doubled(arrived[pl.ds(k * F + f, devices, stride=ROWS), :])
                for f in range(F)
            ],
            axis=1,
        )
        total = total + jnp.dot(pick(LABELS + k), rows, preferred_element_type=jnp.float32)

    rows = jnp.concatenate(
        [doubled(arrived[pl.ds(at, devices, stride=ROWS), :]) for at in (36, 37)], axis=0
    )
    none = jnp.zeros((CX, 2 * devices), jnp.bfloat16)
    sums = []
    for side in (LABELS + CAP, LABELS + 2 * CAP):
        hot = jnp.concatenate(
            [
                jnp.concatenate(
                    [pick(side + k), pick(side + SPLIT + k) if SPLIT + k < CAP else none], axis=1
                )
                for k in range(SPLIT)
            ],
            axis=0,
        )
        found = jnp.dot(hot, rows, preferred_element_type=jnp.float32)
        value = found[:CX]
        for k in range(1, SPLIT):
            value = value + pltpu.roll(found[k * CX : (k + 1) * CX], B - SPAN * k, 1)
        sums.append(value)
    lane = lax.broadcasted_iota(jnp.int32, (CX, B), 1)
    from_before = lane < 0
    for start, width in SPANS:
        from_before |= (lane >= start) & (lane < start + width)
    beside = jnp.where(from_before, sums[0], sums[1])
    own = [total[:, f * B : (f + 1) * B] for f in range(F)]
    for f in range(F):
        flux[f] = own[f]
    own = [own[0], own[1], forcing * (own[2] + steric * own[3])]
    fields = []
    for (start, width), value in zip(SPANS, own):
        moved = pltpu.roll(beside, B - width - start, 1)
        outer = jnp.where((lane >= B - width) | (lane < width), moved, 0.0)
        fields.append(jnp.concatenate([value, outer], axis=1))
    for i, field in enumerate(fields):
        wide[i] = field
    odd = lax.axis_index("atm") % 2 == 1
    outers = [field[:, B:] for field in fields] + [state[i, :, B:] for i in range(4)]
    top, bottom = slice(0, 8), slice(CX - 8, CX)
    for rows, other, message in ((top, bottom, to_pair), (bottom, top, to_beside)):
        packed = jnp.zeros((8, B), jnp.float32)
        for i, outer in enumerate(outers):
            at = 2 * REACH * i
            moved = pltpu.roll(jnp.where(odd, outer[rows], outer[other]), at + REACH, 1)
            packed = jnp.where((lane[:8] >= at) & (lane[:8] < at + 2 * REACH), moved, packed)
        for i, field in enumerate(fields):
            message[i] = jnp.where(odd, field[rows, :B], field[other, :B])
        message[3] = packed


def sum_rows(arrived, state, devices):
    inside = pl.BlockSpec(memory_space=pltpu.VMEM)
    return pl.pallas_call(
        functools.partial(sum_kernel, devices=devices),
        out_shape=(
            jax.ShapeDtypeStruct((F, CX, B), jnp.float32),
            jax.ShapeDtypeStruct((3, CX, 2 * B), jnp.float32),
            jax.ShapeDtypeStruct((4, 8, B), jnp.float32),
            jax.ShapeDtypeStruct((4, 8, B), jnp.float32),
        ),
        in_specs=[inside] * 2,
        out_specs=(inside,) * 4,
        compiler_params=pltpu.CompilerParams(vmem_limit_bytes=32 << 20),
        name="sum_rows",
    )(arrived, state)


def step_kernel(
    state,
    flux,
    wide,
    pair,
    beside,
    state_pair,
    state_beside,
    flux_out,
    height_out,
    zonal_out,
    merid_out,
    sem,
    *,
    lines,
):
    send = pltpu.make_async_copy(flux, flux_out, sem)
    send.start()
    rows = CX + 16
    line = lax.axis_index("atm")
    odd = line % 2 == 1
    has_above = line > 0
    has_below = line < lines - 1

    lane = lax.broadcasted_iota(jnp.int32, (8, B), 1)
    ends = (lane >= B - REACH) | (lane < REACH)

    def chosen(i, by_pair, by_beside, valid):
        return jnp.where(valid, jnp.where(odd, by_pair[i], by_beside[i]), 0.0)

    above = [chosen(i, pair, beside, has_above) for i in range(4)]
    below = [chosen(i, beside, pair, has_below) for i in range(4)]
    above = above[:3] + [chosen(i, state_pair, state_beside, has_above) for i in range(4)] + above[3:]
    below = below[:3] + [chosen(i, state_beside, state_pair, has_below) for i in range(4)] + below[3:]

    def field(i):
        own = wide[i] if i < 3 else state[i - 3]
        by = (B - 2 * REACH * i - REACH) % B
        return jnp.concatenate(
            [
                jnp.concatenate([rows[i], jnp.where(ends, pltpu.roll(rows[7], by, 1), 0.0)], axis=1)
                if n != 1
                else own
                for n, rows in enumerate((above, None, below))
            ],
            axis=0,
        )

    zonal_flux, merid_flux, source = field(0), field(1), field(2)
    height, zonal, merid, depth = field(3), field(4), field(5), field(6)
    inside = depth > 0.0

    def grad_x(a):
        return 0.5 * (pltpu.roll(a, rows - 1, 0) - pltpu.roll(a, 1, 0))

    def grad_y(a):
        return 0.5 * (pltpu.roll(a, 2 * B - 1, 1) - pltpu.roll(a, 1, 1))

    slope = (0.5 * courant) * depth
    zonal_gain, merid_gain = forcing * zonal_flux, forcing * merid_flux

    def diff_x(a):
        return pltpu.roll(a, rows - 1, 0) - pltpu.roll(a, 1, 0)

    def diff_y(a):
        return pltpu.roll(a, 2 * B - 1, 1) - pltpu.roll(a, 1, 1)

    for _ in range(STEPS):
        height = height - slope * (diff_x(zonal) + diff_y(merid)) + source
        new_zonal = (
            (1.0 - damping) * zonal
            - (0.5 * courant) * diff_x(height)
            + coriolis * merid
            + zonal_gain
        )
        new_merid = (
            (1.0 - damping) * merid
            - (0.5 * courant) * diff_y(height)
            - coriolis * zonal
            + merid_gain
        )
        zonal = jnp.where(inside, new_zonal, 0.0)
        merid = jnp.where(inside, new_merid, 0.0)
    height_out[...] = height[8 : 8 + CX, :B]
    zonal_out[...] = zonal[8 : 8 + CX, :B]
    merid_out[...] = merid[8 : 8 + CX, :B]
    send.wait()


def substeps(lines, *args):
    inside = pl.BlockSpec(memory_space=pltpu.VMEM)
    shape = jax.ShapeDtypeStruct((CX, B), jnp.float32)
    return pl.pallas_call(
        functools.partial(step_kernel, lines=lines),
        out_shape=(jax.ShapeDtypeStruct((F, CX, B), jnp.float32),) + (shape,) * 3,
        in_specs=[inside] * 7,
        out_specs=(pl.BlockSpec(memory_space=pltpu.HBM),) + (inside,) * 3,
        scratch_shapes=[pltpu.SemaphoreType.DMA],
        compiler_params=pltpu.CompilerParams(vmem_limit_bytes=32 << 20),
        name="substeps",
    )(*args)


def around(x, axis, by):
    n = lax.axis_size(axis)
    return lax.ppermute(x, axis, [(i, (i + by) % n) for i in range(n)])


def with_pair(x):
    return lax.ppermute(x, "atm", [(i, i ^ 1) for i in range(lax.axis_size("atm"))])


def with_beside(x):
    lines, columns = lax.axis_size("atm"), lax.axis_size("ocn")
    partners = []
    for i in range(lines):
        other = i + 1 if i % 2 else i - 1
        for j in range(columns):
            here = i * columns + j
            partners.append(
                (here, other * columns + j if 0 <= other < lines else here - j + (j ^ 1))
            )
    return lax.ppermute(x, AXES, partners)


def on_device(
    source_flux,
    remap_weights,
    source_block,
    owner_device,
    target_row,
    sea_height,
    u_velocity,
    v_velocity,
    ocean_depth,
):
    ocn = lax.axis_size("ocn")
    devices = lax.axis_size("atm") * ocn
    messages = pack(
        owner_device.T, target_row, source_block, source_flux, remap_weights, devices, ocn
    )
    arrived = lax.all_to_all(
        messages.reshape(-1, 1, B), AXES, split_axis=0, concat_axis=0, tiled=True
    ).reshape(-1, B)

    column = lax.axis_index("ocn")
    lines = lax.axis_size("atm")
    state = jnp.stack([sea_height, u_velocity, v_velocity, ocean_depth])
    state, messages = lax.optimization_barrier((state, messages))
    odd = lax.axis_index("atm") % 2 == 1
    firsts, lasts = state[:, :8], state[:, CX - 8 :]
    state_pair = with_pair(jnp.where(odd, firsts, lasts))
    state_beside = with_beside(jnp.where(odd, lasts, firsts))
    before = around(state[:, :, B - REACH :], "ocn", 1)
    after = around(state[:, :, :REACH], "ocn", -1)
    before = jnp.where(column > 0, before, 0.0)
    after = jnp.where(column < ocn - 1, after, 0.0)
    gap = jnp.zeros((4, CX, B - 2 * REACH), jnp.float32)
    state = jnp.concatenate([state, after, gap, before], axis=2)

    flux, wide, to_pair, to_beside = sum_rows(arrived, state, devices)
    pair = with_pair(to_pair)
    beside = with_beside(to_beside)
    return substeps(lines, state, flux, wide, pair, beside, state_pair, state_beside)


def solution(mesh):
    placed = (
        P(None, AXES),
        P(AXES, None, None),
        P(AXES),
        P(AXES, None),
        P(AXES),
        P("atm", "ocn"),
        P("atm", "ocn"),
        P("atm", "ocn"),
        P("atm", "ocn"),
    )
    return jax.shard_map(
        on_device,
        mesh=mesh,
        in_specs=placed,
        out_specs=(P(None, "atm", "ocn"), P("atm", "ocn"), P("atm", "ocn"), P("atm", "ocn")),
        check_vma=False,
    )
```

```python
import functools
import math

import jax
import jax.numpy as jnp
from jax import lax
from jax.experimental import pallas as pl
from jax.experimental.pallas import tpu as pltpu
from jax.sharding import Mesh, PartitionSpec as P

CX = 64
STEPS = 3
F = 4
B = 128
CAP = 9
ROWS = 38
REACH = 6
SPANS = ((0, 3), (6, 4), (14, 5))
SPAN = 24
SPLIT = 5
LABELS = 96
CHUNKS = 24

courant = 0.5
forcing = 0.3
coriolis = 0.2
damping = 0.05
steric = 0.5

SIZES = (4, 4, 2, 4)
AXES = ("x", "y", "core", "ocn")
ATM = AXES[:3]
PEERS = ("core", "ocn", "y", "x")


def pack_kernel(
    owner_h,
    target_h,
    block_h,
    src_h,
    weights_h,
    out,
    weights,
    lhs,
    src,
    owner,
    target,
    block,
    row_of,
    first_row,
    built,
    sems,
    small_sems,
    out_sems,
    *,
    order,
    stride,
    ocn,
):
    total = weights.shape[0]
    per = total // CHUNKS
    smalls = [
        pltpu.make_async_copy(a, b, small_sems.at[i])
        for i, (a, b) in enumerate(
            ((src_h, src), (owner_h, owner), (target_h, target), (block_h, block))
        )
    ]
    for copy in smalls:
        copy.start(priority=0)
    copies = [
        pltpu.make_async_copy(
            weights_h.at[pl.ds(c * per, per)], weights.at[pl.ds(c * per, per)], sems.at[c]
        )
        for c in range(CHUNKS)
    ]
    for copy in copies:
        copy.start(priority=1)
    devices = len(order)
    lane = lax.broadcasted_iota(jnp.int32, (devices, B), 1)
    built[...] = jnp.zeros(built.shape, jnp.float32)
    built[pl.ds(37, devices, stride=ROWS), :] = jnp.where(lane < LABELS, 0.0, -1.0)
    for o, at in enumerate(order):
        row_of[o] = at * ROWS
        first_row[o] = at * ROWS
    smalls[0].wait()
    zero = jnp.zeros((F, B), jnp.float32)
    for b in range(src.shape[1] // B):
        value = src[:, b * B : (b + 1) * B].astype(jnp.float32)
        for j in range(4):
            parts = [zero] * 4
            parts[j] = value
            lhs[j, b] = jnp.concatenate(parts, 0).astype(jnp.bfloat16)
    for copy in smalls[1:]:
        copy.wait()
    slot = F * (lax.broadcasted_iota(jnp.int32, (1, B), 1) - LABELS)
    for c in range(CHUNKS):
        copies[c].wait()
        for w in range(c * per, (c + 1) * per, 4):
            left = jnp.concatenate([lhs[j, block[w + j]] for j in range(4)], axis=1)
            right = weights[w : w + 4].reshape(4 * B, B)
            rows = jnp.dot(left, right, preferred_element_type=jnp.float32)
            for j in range(4):
                o = owner[0, w + j]
                row = row_of[o]
                first = first_row[o]
                row_of[o] = row + F
                built[pl.ds(row, F), :] = rows[F * j : F * (j + 1)]
                name = jnp.full((1, B), target[w + j].astype(jnp.float32))
                pltpu.store(built.at[pl.ds(first + 37, 1), :], name, mask=slot == row - first)

    group = stride * ocn
    lane = lax.broadcasted_iota(jnp.int32, (group, B), 1)
    place = lax.broadcasted_iota(jnp.int32, (group, B), 0) // stride
    sends = []
    for g in range(devices // group):
        base = g * group * ROWS
        edge = [jnp.zeros((group, B), jnp.float32) for _ in range(2)]
        from_before = [lane < 0, lane < 0]
        for k in range(CAP):
            part = k // SPLIT
            rows = [built[pl.ds(base + k * F + f, group, stride=ROWS), :] for f in range(F)]
            rows = [rows[0], rows[1], forcing * (rows[2] + steric * rows[3])]
            for (start, width), value in zip(SPANS, rows):
                at = (k % SPLIT) * SPAN + start
                moved = pltpu.roll(value, (at - (B - width)) % B, 1)
                edge[part] = jnp.where((lane >= at) & (lane < at + 2 * width), moved, edge[part])
                from_before[part] |= (lane >= at) & (lane < at + width)
        sides = [
            jnp.where(mask, pltpu.roll(value, stride, 0), pltpu.roll(value, group - stride, 0))
            for mask, value in zip(from_before, edge)
        ]
        own = built[pl.ds(base + 37, group, stride=ROWS), :]
        before = jnp.where(place > 0, pltpu.roll(own, stride, 0), -1.0)
        after = jnp.where(place < ocn - 1, pltpu.roll(own, group - stride, 0), -1.0)
        for i, names in enumerate((own, before, after)):
            at = LABELS + CAP * i
            names = pltpu.roll(names, CAP * i, 1) if i else names
            sides[1] = jnp.where((lane >= at) & (lane < at + CAP), names, sides[1])
        built[pl.ds(base + 36, group, stride=ROWS), :] = sides[0]
        built[pl.ds(base + 37, group, stride=ROWS), :] = sides[1]
        span = pl.ds(base, group * ROWS)
        send = pltpu.make_async_copy(built.at[span], out.at[span], out_sems.at[g])
        send.start()
        sends.append(send)
    for send in sends:
        send.wait()


def pack(owner, target, block, src, weights):
    total = weights.shape[0]
    sizes = [lax.axis_size(axis) for axis in AXES]
    devices = math.prod(sizes)
    order = []
    for o in range(devices):
        at = 0
        for axis in PEERS:
            i = AXES.index(axis)
            at = at * sizes[i] + o // math.prod(sizes[i + 1 :]) % sizes[i]
        order.append(at)
    stride, ocn = sizes[0] * sizes[1], sizes[3]
    here = pl.BlockSpec(memory_space=pltpu.HBM)
    return pl.pallas_call(
        functools.partial(pack_kernel, order=tuple(order), stride=stride, ocn=ocn),
        out_shape=jax.ShapeDtypeStruct((devices * ROWS, B), jnp.float32),
        in_specs=[here] * 5,
        out_specs=here,
        scratch_shapes=[
            pltpu.VMEM(weights.shape, jnp.bfloat16),
            pltpu.VMEM((4, src.shape[1] // B, 4 * F, B), jnp.bfloat16),
            pltpu.VMEM(src.shape, jnp.bfloat16),
            pltpu.SMEM((1, total), jnp.int32),
            pltpu.SMEM((total,), jnp.int32),
            pltpu.SMEM((total,), jnp.int32),
            pltpu.SMEM((devices,), jnp.int32),
            pltpu.SMEM((devices,), jnp.int32),
            pltpu.VMEM((devices * ROWS, B), jnp.float32),
            pltpu.SemaphoreType.DMA((CHUNKS,)),
            pltpu.SemaphoreType.DMA((4,)),
            pltpu.SemaphoreType.DMA((devices // (stride * ocn),)),
        ],
        compiler_params=pltpu.CompilerParams(vmem_limit_bytes=60 << 20),
        cost_estimate=pl.CostEstimate(
            flops=2 * F * weights.size, bytes_accessed=2 * weights.size, transcendentals=0
        ),
        name="remap_pack",
    )(owner, target, block, src, weights)


def doubled(value):
    high = value.astype(jnp.bfloat16)
    low = (value - high.astype(jnp.float32)).astype(jnp.bfloat16)
    return jnp.concatenate([high, low], axis=0)


def sum_kernel(arrived, state, flux, wide, to_pair, to_beside, *, devices):
    names = arrived[pl.ds(37, devices, stride=ROWS), :].T
    row = lax.broadcasted_iota(jnp.int32, (CX, devices), 0).astype(jnp.float32)

    def pick(lane):
        hot = (row == names[lane : lane + 1, :]).astype(jnp.bfloat16)
        return jnp.concatenate([hot, hot], axis=1)

    total = jnp.zeros((CX, F * B), jnp.float32)
    for k in range(CAP):
        rows = jnp.concatenate(
            [
                doubled(arrived[pl.ds(k * F + f, devices, stride=ROWS), :])
                for f in range(F)
            ],
            axis=1,
        )
        total = total + jnp.dot(pick(LABELS + k), rows, preferred_element_type=jnp.float32)

    rows = jnp.concatenate(
        [doubled(arrived[pl.ds(at, devices, stride=ROWS), :]) for at in (36, 37)], axis=0
    )
    none = jnp.zeros((CX, 2 * devices), jnp.bfloat16)
    sums = []
    for side in (LABELS + CAP, LABELS + 2 * CAP):
        hot = jnp.concatenate(
            [
                jnp.concatenate(
                    [pick(side + k), pick(side + SPLIT + k) if SPLIT + k < CAP else none], axis=1
                )
                for k in range(SPLIT)
            ],
            axis=0,
        )
        found = jnp.dot(hot, rows, preferred_element_type=jnp.float32)
        value = found[:CX]
        for k in range(1, SPLIT):
            value = value + pltpu.roll(found[k * CX : (k + 1) * CX], B - SPAN * k, 1)
        sums.append(value)
    lane = lax.broadcasted_iota(jnp.int32, (CX, B), 1)
    from_before = lane < 0
    for start, width in SPANS:
        from_before |= (lane >= start) & (lane < start + width)
    beside = jnp.where(from_before, sums[0], sums[1])
    own = [total[:, f * B : (f + 1) * B] for f in range(F)]
    for f in range(F):
        flux[f] = own[f]
    own = [own[0], own[1], forcing * (own[2] + steric * own[3])]
    fields = []
    for (start, width), value in zip(SPANS, own):
        moved = pltpu.roll(beside, B - width - start, 1)
        outer = jnp.where((lane >= B - width) | (lane < width), moved, 0.0)
        fields.append(jnp.concatenate([value, outer], axis=1))
    for i, field in enumerate(fields):
        wide[i] = field
    odd = lax.axis_index("core") == 1
    outers = [field[:, B:] for field in fields] + [state[i, :, B:] for i in range(4)]
    top, bottom = slice(0, 8), slice(CX - 8, CX)
    for rows, other, message in ((top, bottom, to_pair), (bottom, top, to_beside)):
        packed = jnp.zeros((8, B), jnp.float32)
        for i, outer in enumerate(outers):
            at = 2 * REACH * i
            moved = pltpu.roll(jnp.where(odd, outer[rows], outer[other]), at + REACH, 1)
            packed = jnp.where((lane[:8] >= at) & (lane[:8] < at + 2 * REACH), moved, packed)
        for i, field in enumerate(fields):
            message[i] = jnp.where(odd, field[rows, :B], field[other, :B])
        message[3] = packed


def sum_rows(arrived, state, devices):
    inside = pl.BlockSpec(memory_space=pltpu.VMEM)
    return pl.pallas_call(
        functools.partial(sum_kernel, devices=devices),
        out_shape=(
            jax.ShapeDtypeStruct((F, CX, B), jnp.float32),
            jax.ShapeDtypeStruct((3, CX, 2 * B), jnp.float32),
            jax.ShapeDtypeStruct((4, 8, B), jnp.float32),
            jax.ShapeDtypeStruct((4, 8, B), jnp.float32),
        ),
        in_specs=[inside] * 2,
        out_specs=(inside,) * 4,
        compiler_params=pltpu.CompilerParams(vmem_limit_bytes=32 << 20),
        name="sum_rows",
    )(arrived, state)


def step_kernel(
    state,
    flux,
    wide,
    pair,
    beside,
    state_pair,
    state_beside,
    flux_out,
    height_out,
    zonal_out,
    merid_out,
    sem,
    *,
    lines,
):
    send = pltpu.make_async_copy(flux, flux_out, sem)
    send.start()
    rows = CX + 16
    core = lax.axis_index("core")
    line = (lax.axis_index("x") * lax.axis_size("y") + lax.axis_index("y")) * 2 + core
    odd = core == 1
    has_above = line > 0
    has_below = line < lines - 1

    lane = lax.broadcasted_iota(jnp.int32, (8, B), 1)
    ends = (lane >= B - REACH) | (lane < REACH)

    def chosen(i, by_pair, by_beside, valid):
        return jnp.where(valid, jnp.where(odd, by_pair[i], by_beside[i]), 0.0)

    above = [chosen(i, pair, beside, has_above) for i in range(4)]
    below = [chosen(i, beside, pair, has_below) for i in range(4)]
    above = above[:3] + [chosen(i, state_pair, state_beside, has_above) for i in range(4)] + above[3:]
    below = below[:3] + [chosen(i, state_beside, state_pair, has_below) for i in range(4)] + below[3:]

    def field(i):
        own = wide[i] if i < 3 else state[i - 3]
        by = (B - 2 * REACH * i - REACH) % B
        return jnp.concatenate(
            [
                jnp.concatenate([rows[i], jnp.where(ends, pltpu.roll(rows[7], by, 1), 0.0)], axis=1)
                if n != 1
                else own
                for n, rows in enumerate((above, None, below))
            ],
            axis=0,
        )

    zonal_flux, merid_flux, source = field(0), field(1), field(2)
    height, zonal, merid, depth = field(3), field(4), field(5), field(6)
    inside = depth > 0.0

    def grad_x(a):
        return 0.5 * (pltpu.roll(a, rows - 1, 0) - pltpu.roll(a, 1, 0))

    def grad_y(a):
        return 0.5 * (pltpu.roll(a, 2 * B - 1, 1) - pltpu.roll(a, 1, 1))

    slope = (0.5 * courant) * depth
    zonal_gain, merid_gain = forcing * zonal_flux, forcing * merid_flux

    def diff_x(a):
        return pltpu.roll(a, rows - 1, 0) - pltpu.roll(a, 1, 0)

    def diff_y(a):
        return pltpu.roll(a, 2 * B - 1, 1) - pltpu.roll(a, 1, 1)

    for _ in range(STEPS):
        height = height - slope * (diff_x(zonal) + diff_y(merid)) + source
        new_zonal = (
            (1.0 - damping) * zonal
            - (0.5 * courant) * diff_x(height)
            + coriolis * merid
            + zonal_gain
        )
        new_merid = (
            (1.0 - damping) * merid
            - (0.5 * courant) * diff_y(height)
            - coriolis * zonal
            + merid_gain
        )
        zonal = jnp.where(inside, new_zonal, 0.0)
        merid = jnp.where(inside, new_merid, 0.0)
    height_out[...] = height[8 : 8 + CX, :B]
    zonal_out[...] = zonal[8 : 8 + CX, :B]
    merid_out[...] = merid[8 : 8 + CX, :B]
    send.wait()


def substeps(lines, *args):
    inside = pl.BlockSpec(memory_space=pltpu.VMEM)
    shape = jax.ShapeDtypeStruct((CX, B), jnp.float32)
    return pl.pallas_call(
        functools.partial(step_kernel, lines=lines),
        out_shape=(jax.ShapeDtypeStruct((F, CX, B), jnp.float32),) + (shape,) * 3,
        in_specs=[inside] * 7,
        out_specs=(pl.BlockSpec(memory_space=pltpu.HBM),) + (inside,) * 3,
        scratch_shapes=[pltpu.SemaphoreType.DMA],
        compiler_params=pltpu.CompilerParams(vmem_limit_bytes=32 << 20),
        name="substeps",
    )(*args)


def around(x, axis, by):
    n = lax.axis_size(axis)
    return lax.ppermute(x, axis, [(i, (i + by) % n) for i in range(n)])


def packed(x):
    return x.transpose(0, 2, 1).reshape(-1, B)


def unpacked(x):
    return x.reshape(4, REACH, CX).transpose(0, 2, 1)


def with_pair(x):
    return lax.ppermute(x, ATM, [(i, i ^ 1) for i in range(lax.axis_size(ATM))])


def with_beside(x):
    lines, columns = lax.axis_size(ATM), lax.axis_size("ocn")
    partners = []
    for i in range(lines):
        other = i + 1 if i % 2 else i - 1
        for j in range(columns):
            here = i * columns + j
            partners.append(
                (here, other * columns + j if 0 <= other < lines else here - j + (j ^ 1))
            )
    return lax.ppermute(x, AXES, partners)


def on_device(
    source_flux,
    remap_weights,
    source_block,
    owner_device,
    target_row,
    sea_height,
    u_velocity,
    v_velocity,
    ocean_depth,
):
    ocn = lax.axis_size("ocn")
    lines = lax.axis_size(ATM)
    devices = lines * ocn
    messages = pack(
        owner_device.T, target_row, source_block, source_flux, remap_weights
    )
    arrived = lax.all_to_all(
        messages.reshape(-1, 1, B), PEERS, split_axis=0, concat_axis=0, tiled=True
    ).reshape(-1, B)

    column = lax.axis_index("ocn")
    state = jnp.stack([sea_height, u_velocity, v_velocity, ocean_depth])
    state, messages = lax.optimization_barrier((state, messages))
    odd = lax.axis_index("core") == 1
    firsts, lasts = state[:, :8], state[:, CX - 8 :]
    state_pair = with_pair(jnp.where(odd, firsts, lasts))
    state_beside = with_beside(jnp.where(odd, lasts, firsts))
    before = unpacked(around(packed(state[:, :, B - REACH :]), "ocn", 1))
    after = unpacked(around(packed(state[:, :, :REACH]), "ocn", -1))
    before = jnp.where(column > 0, before, 0.0)
    after = jnp.where(column < ocn - 1, after, 0.0)
    gap = jnp.zeros((4, CX, B - 2 * REACH), jnp.float32)
    state = jnp.concatenate([state, after, gap, before], axis=2)

    flux, wide, to_pair, to_beside = sum_rows(arrived, state, devices)
    pair = with_pair(to_pair)
    beside = with_beside(to_beside)
    return substeps(lines, state, flux, wide, pair, beside, state_pair, state_beside)


def solution(mesh):
    mesh = Mesh(mesh.devices.reshape(SIZES), AXES)
    cells = P(ATM, "ocn")
    placed = (
        P(None, AXES),
        P(AXES, None, None),
        P(AXES),
        P(AXES, None),
        P(AXES),
        cells,
        cells,
        cells,
        cells,
    )
    return jax.shard_map(
        on_device,
        mesh=mesh,
        in_specs=placed,
        out_specs=(P(None, ATM, "ocn"), cells, cells, cells),
        check_vma=False,
    )
```

```python
import functools
import math

import jax
import jax.numpy as jnp
from jax import lax
from jax.experimental import pallas as pl
from jax.experimental.pallas import tpu as pltpu
from jax.sharding import Mesh, PartitionSpec as P

CX = 64
STEPS = 3
F = 4
B = 128
CAP = 9
ROWS = 38
REACH = 6
SPANS = ((0, 3), (6, 4), (14, 5))
SPAN = 24
SPLIT = 5
LABELS = 96
CHUNKS = 24

courant = 0.5
forcing = 0.3
coriolis = 0.2
damping = 0.05
steric = 0.5

SIZES = (4, 4, 2, 4)
AXES = ("x", "y", "core", "ocn")
ATM = AXES[:3]
PEERS = ("core", "ocn", "y", "x")


def pack_kernel(
    owner_h,
    target_h,
    block_h,
    src_h,
    weights_h,
    out,
    weights,
    lhs,
    src,
    owner,
    target,
    block,
    row_of,
    first_row,
    built,
    sems,
    small_sems,
    out_sems,
    *,
    order,
    stride,
    ocn,
):
    total = weights.shape[0]
    per = total // CHUNKS
    smalls = [
        pltpu.make_async_copy(a, b, small_sems.at[i])
        for i, (a, b) in enumerate(
            ((src_h, src), (owner_h, owner), (target_h, target), (block_h, block))
        )
    ]
    for copy in smalls:
        copy.start(priority=0)
    copies = [
        pltpu.make_async_copy(
            weights_h.at[pl.ds(c * per, per)], weights.at[pl.ds(c * per, per)], sems.at[c]
        )
        for c in range(CHUNKS)
    ]
    for copy in copies:
        copy.start(priority=1)
    devices = len(order)
    lane = lax.broadcasted_iota(jnp.int32, (devices, B), 1)
    built[...] = jnp.zeros(built.shape, jnp.float32)
    built[pl.ds(37, devices, stride=ROWS), :] = jnp.where(lane < LABELS, 0.0, -1.0)
    for o, at in enumerate(order):
        row_of[o] = at * ROWS
        first_row[o] = at * ROWS
    smalls[0].wait()
    zero = jnp.zeros((F, B), jnp.float32)
    for b in range(src.shape[1] // B):
        value = src[:, b * B : (b + 1) * B].astype(jnp.float32)
        for j in range(4):
            parts = [zero] * 4
            parts[j] = value
            lhs[j, b] = jnp.concatenate(parts, 0).astype(jnp.bfloat16)
    for copy in smalls[1:]:
        copy.wait()
    slot = F * (lax.broadcasted_iota(jnp.int32, (1, B), 1) - LABELS)
    for c in range(CHUNKS):
        copies[c].wait()
        for w in range(c * per, (c + 1) * per, 4):
            left = jnp.concatenate([lhs[j, block[w + j]] for j in range(4)], axis=1)
            right = weights[w : w + 4].reshape(4 * B, B)
            rows = jnp.dot(left, right, preferred_element_type=jnp.float32)
            for j in range(4):
                o = owner[0, w + j]
                row = row_of[o]
                first = first_row[o]
                row_of[o] = row + F
                built[pl.ds(row, F), :] = rows[F * j : F * (j + 1)]
                name = jnp.full((1, B), target[w + j].astype(jnp.float32))
                pltpu.store(built.at[pl.ds(first + 37, 1), :], name, mask=slot == row - first)

    group = stride * ocn
    lane = lax.broadcasted_iota(jnp.int32, (group, B), 1)
    place = lax.broadcasted_iota(jnp.int32, (group, B), 0) // stride
    sends = []
    for g in range(devices // group):
        base = g * group * ROWS
        edge = [jnp.zeros((group, B), jnp.float32) for _ in range(2)]
        from_before = [lane < 0, lane < 0]
        for k in range(CAP):
            part = k // SPLIT
            rows = [built[pl.ds(base + k * F + f, group, stride=ROWS), :] for f in range(F)]
            rows = [rows[0], rows[1], forcing * (rows[2] + steric * rows[3])]
            for (start, width), value in zip(SPANS, rows):
                at = (k % SPLIT) * SPAN + start
                moved = pltpu.roll(value, (at - (B - width)) % B, 1)
                edge[part] = jnp.where((lane >= at) & (lane < at + 2 * width), moved, edge[part])
                from_before[part] |= (lane >= at) & (lane < at + width)
        sides = [
            jnp.where(mask, pltpu.roll(value, stride, 0), pltpu.roll(value, group - stride, 0))
            for mask, value in zip(from_before, edge)
        ]
        own = built[pl.ds(base + 37, group, stride=ROWS), :]
        before = jnp.where(place > 0, pltpu.roll(own, stride, 0), -1.0)
        after = jnp.where(place < ocn - 1, pltpu.roll(own, group - stride, 0), -1.0)
        for i, names in enumerate((own, before, after)):
            at = LABELS + CAP * i
            names = pltpu.roll(names, CAP * i, 1) if i else names
            sides[1] = jnp.where((lane >= at) & (lane < at + CAP), names, sides[1])
        built[pl.ds(base + 36, group, stride=ROWS), :] = sides[0]
        built[pl.ds(base + 37, group, stride=ROWS), :] = sides[1]
        span = pl.ds(base, group * ROWS)
        send = pltpu.make_async_copy(built.at[span], out.at[span], out_sems.at[g])
        send.start()
        sends.append(send)
    for send in sends:
        send.wait()


def pack(owner, target, block, src, weights):
    total = weights.shape[0]
    sizes = [lax.axis_size(axis) for axis in AXES]
    devices = math.prod(sizes)
    order = []
    for o in range(devices):
        at = 0
        for axis in PEERS:
            i = AXES.index(axis)
            at = at * sizes[i] + o // math.prod(sizes[i + 1 :]) % sizes[i]
        order.append(at)
    stride, ocn = sizes[0] * sizes[1], sizes[3]
    here = pl.BlockSpec(memory_space=pltpu.HBM)
    return pl.pallas_call(
        functools.partial(pack_kernel, order=tuple(order), stride=stride, ocn=ocn),
        out_shape=jax.ShapeDtypeStruct((devices * ROWS, B), jnp.float32),
        in_specs=[here] * 5,
        out_specs=here,
        scratch_shapes=[
            pltpu.VMEM(weights.shape, jnp.bfloat16),
            pltpu.VMEM((4, src.shape[1] // B, 4 * F, B), jnp.bfloat16),
            pltpu.VMEM(src.shape, jnp.bfloat16),
            pltpu.SMEM((1, total), jnp.int32),
            pltpu.SMEM((total,), jnp.int32),
            pltpu.SMEM((total,), jnp.int32),
            pltpu.SMEM((devices,), jnp.int32),
            pltpu.SMEM((devices,), jnp.int32),
            pltpu.VMEM((devices * ROWS, B), jnp.float32),
            pltpu.SemaphoreType.DMA((CHUNKS,)),
            pltpu.SemaphoreType.DMA((4,)),
            pltpu.SemaphoreType.DMA((devices // (stride * ocn),)),
        ],
        compiler_params=pltpu.CompilerParams(vmem_limit_bytes=60 << 20),
        cost_estimate=pl.CostEstimate(
            flops=2 * F * weights.size, bytes_accessed=2 * weights.size, transcendentals=0
        ),
        name="remap_pack",
    )(owner, target, block, src, weights)


def doubled(value):
    high = value.astype(jnp.bfloat16)
    low = (value - high.astype(jnp.float32)).astype(jnp.bfloat16)
    return jnp.concatenate([high, low], axis=0)


def sum_kernel(arrived, state, flux, wide, to_pair, to_beside, *, devices):
    names = arrived[pl.ds(37, devices, stride=ROWS), :].T
    row = lax.broadcasted_iota(jnp.int32, (CX, devices), 0).astype(jnp.float32)

    def pick(lane):
        hot = (row == names[lane : lane + 1, :]).astype(jnp.bfloat16)
        return jnp.concatenate([hot, hot], axis=1)

    total = jnp.zeros((CX, F * B), jnp.float32)
    for k in range(CAP):
        rows = jnp.concatenate(
            [
                doubled(arrived[pl.ds(k * F + f, devices, stride=ROWS), :])
                for f in range(F)
            ],
            axis=1,
        )
        total = total + jnp.dot(pick(LABELS + k), rows, preferred_element_type=jnp.float32)

    rows = jnp.concatenate(
        [doubled(arrived[pl.ds(at, devices, stride=ROWS), :]) for at in (36, 37)], axis=0
    )
    none = jnp.zeros((CX, 2 * devices), jnp.bfloat16)
    sums = []
    for side in (LABELS + CAP, LABELS + 2 * CAP):
        hot = jnp.concatenate(
            [
                jnp.concatenate(
                    [pick(side + k), pick(side + SPLIT + k) if SPLIT + k < CAP else none], axis=1
                )
                for k in range(SPLIT)
            ],
            axis=0,
        )
        found = jnp.dot(hot, rows, preferred_element_type=jnp.float32)
        value = found[:CX]
        for k in range(1, SPLIT):
            value = value + pltpu.roll(found[k * CX : (k + 1) * CX], B - SPAN * k, 1)
        sums.append(value)
    lane = lax.broadcasted_iota(jnp.int32, (CX, B), 1)
    from_before = lane < 0
    for start, width in SPANS:
        from_before |= (lane >= start) & (lane < start + width)
    beside = jnp.where(from_before, sums[0], sums[1])
    own = [total[:, f * B : (f + 1) * B] for f in range(F)]
    for f in range(F):
        flux[f] = own[f]
    own = [own[0], own[1], forcing * (own[2] + steric * own[3])]
    fields = []
    for (start, width), value in zip(SPANS, own):
        moved = pltpu.roll(beside, B - width - start, 1)
        outer = jnp.where((lane >= B - width) | (lane < width), moved, 0.0)
        fields.append(jnp.concatenate([value, outer], axis=1))
    for i, field in enumerate(fields):
        wide[i] = field
    odd = lax.axis_index("core") == 1
    outers = [field[:, B:] for field in fields] + [state[i, :, B:] for i in range(4)]
    top, bottom = slice(0, 8), slice(CX - 8, CX)
    for rows, other, message in ((top, bottom, to_pair), (bottom, top, to_beside)):
        packed = jnp.zeros((8, B), jnp.float32)
        for i, outer in enumerate(outers):
            at = 2 * REACH * i
            moved = pltpu.roll(jnp.where(odd, outer[rows], outer[other]), at + REACH, 1)
            packed = jnp.where((lane[:8] >= at) & (lane[:8] < at + 2 * REACH), moved, packed)
        for i, field in enumerate(fields):
            message[i] = jnp.where(odd, field[rows, :B], field[other, :B])
        message[3] = packed


def sum_rows(arrived, state, devices):
    inside = pl.BlockSpec(memory_space=pltpu.VMEM)
    return pl.pallas_call(
        functools.partial(sum_kernel, devices=devices),
        out_shape=(
            jax.ShapeDtypeStruct((F, CX, B), jnp.float32),
            jax.ShapeDtypeStruct((3, CX, 2 * B), jnp.float32),
            jax.ShapeDtypeStruct((4, 8, B), jnp.float32),
            jax.ShapeDtypeStruct((4, 8, B), jnp.float32),
        ),
        in_specs=[inside] * 2,
        out_specs=(inside,) * 4,
        compiler_params=pltpu.CompilerParams(vmem_limit_bytes=32 << 20),
        name="sum_rows",
    )(arrived, state)


def step_kernel(
    state,
    flux,
    wide,
    pair,
    beside,
    state_pair,
    state_beside,
    flux_out,
    height_out,
    zonal_out,
    merid_out,
    sem,
    *,
    lines,
):
    send = pltpu.make_async_copy(flux, flux_out, sem)
    send.start()
    rows = CX + 16
    core = lax.axis_index("core")
    line = (lax.axis_index("x") * lax.axis_size("y") + lax.axis_index("y")) * 2 + core
    odd = core == 1
    has_above = line > 0
    has_below = line < lines - 1

    lane = lax.broadcasted_iota(jnp.int32, (8, B), 1)
    ends = (lane >= B - REACH) | (lane < REACH)

    def chosen(i, by_pair, by_beside, valid):
        return jnp.where(valid, jnp.where(odd, by_pair[i], by_beside[i]), 0.0)

    above = [chosen(i, pair, beside, has_above) for i in range(4)]
    below = [chosen(i, beside, pair, has_below) for i in range(4)]
    above = above[:3] + [chosen(i, state_pair, state_beside, has_above) for i in range(4)] + above[3:]
    below = below[:3] + [chosen(i, state_beside, state_pair, has_below) for i in range(4)] + below[3:]

    def field(i):
        own = wide[i] if i < 3 else state[i - 3]
        by = (B - 2 * REACH * i - REACH) % B
        return jnp.concatenate(
            [
                jnp.concatenate([rows[i], jnp.where(ends, pltpu.roll(rows[7], by, 1), 0.0)], axis=1)
                if n != 1
                else own
                for n, rows in enumerate((above, None, below))
            ],
            axis=0,
        )

    zonal_flux, merid_flux, source = field(0), field(1), field(2)
    height, zonal, merid, depth = field(3), field(4), field(5), field(6)
    inside = depth > 0.0

    def grad_x(a):
        return 0.5 * (pltpu.roll(a, rows - 1, 0) - pltpu.roll(a, 1, 0))

    def grad_y(a):
        return 0.5 * (pltpu.roll(a, 2 * B - 1, 1) - pltpu.roll(a, 1, 1))

    slope = (0.5 * courant) * depth
    zonal_gain, merid_gain = forcing * zonal_flux, forcing * merid_flux

    def diff_x(a):
        return pltpu.roll(a, rows - 1, 0) - pltpu.roll(a, 1, 0)

    def diff_y(a):
        return pltpu.roll(a, 2 * B - 1, 1) - pltpu.roll(a, 1, 1)

    for _ in range(STEPS - 1):
        height = height - slope * (diff_x(zonal) + diff_y(merid)) + source
        new_zonal = (
            (1.0 - damping) * zonal
            - (0.5 * courant) * diff_x(height)
            + coriolis * merid
            + zonal_gain
        )
        new_merid = (
            (1.0 - damping) * merid
            - (0.5 * courant) * diff_y(height)
            - coriolis * zonal
            + merid_gain
        )
        zonal = jnp.where(inside, new_zonal, 0.0)
        merid = jnp.where(inside, new_merid, 0.0)
    height = height - slope * (diff_x(zonal) + diff_y(merid)) + source
    own = (slice(8, 8 + CX), slice(0, B))
    height_out[...] = height[own]
    zonal_out[...] = (
        (1.0 - damping) * zonal[own]
        - (0.5 * courant) * diff_x(height[:, :B])[own]
        + coriolis * merid[own]
        + zonal_gain[own]
    )
    merid_out[...] = (
        (1.0 - damping) * merid[own]
        - (0.5 * courant) * diff_y(height[8 : 8 + CX])[:, :B]
        - coriolis * zonal[own]
        + merid_gain[own]
    )
    send.wait()


def substeps(lines, *args):
    inside = pl.BlockSpec(memory_space=pltpu.VMEM)
    shape = jax.ShapeDtypeStruct((CX, B), jnp.float32)
    return pl.pallas_call(
        functools.partial(step_kernel, lines=lines),
        out_shape=(jax.ShapeDtypeStruct((F, CX, B), jnp.float32),) + (shape,) * 3,
        in_specs=[inside] * 7,
        out_specs=(pl.BlockSpec(memory_space=pltpu.HBM),) + (inside,) * 3,
        scratch_shapes=[pltpu.SemaphoreType.DMA],
        compiler_params=pltpu.CompilerParams(vmem_limit_bytes=32 << 20),
        name="substeps",
    )(*args)


def around(x, axis, by):
    n = lax.axis_size(axis)
    return lax.ppermute(x, axis, [(i, (i + by) % n) for i in range(n)])


def packed(x):
    return x.transpose(0, 2, 1).reshape(-1, B)


def unpacked(x):
    return x.reshape(4, REACH, CX).transpose(0, 2, 1)


def with_pair(x):
    return lax.ppermute(x, ATM, [(i, i ^ 1) for i in range(lax.axis_size(ATM))])


def with_beside(x):
    lines, columns = lax.axis_size(ATM), lax.axis_size("ocn")
    partners = []
    for i in range(lines):
        other = i + 1 if i % 2 else i - 1
        for j in range(columns):
            here = i * columns + j
            partners.append(
                (here, other * columns + j if 0 <= other < lines else here - j + (j ^ 1))
            )
    return lax.ppermute(x, AXES, partners)


def on_device(
    source_flux,
    remap_weights,
    source_block,
    owner_device,
    target_row,
    sea_height,
    u_velocity,
    v_velocity,
    ocean_depth,
):
    ocn = lax.axis_size("ocn")
    lines = lax.axis_size(ATM)
    devices = lines * ocn
    messages = pack(
        owner_device.T, target_row, source_block, source_flux, remap_weights
    )
    arrived = lax.all_to_all(
        messages.reshape(-1, 1, B), PEERS, split_axis=0, concat_axis=0, tiled=True
    ).reshape(-1, B)

    column = lax.axis_index("ocn")
    state = jnp.stack([sea_height, u_velocity, v_velocity, ocean_depth])
    state, messages = lax.optimization_barrier((state, messages))
    odd = lax.axis_index("core") == 1
    firsts, lasts = state[:, :8], state[:, CX - 8 :]
    state_pair = with_pair(jnp.where(odd, firsts, lasts))
    state_beside = with_beside(jnp.where(odd, lasts, firsts))
    before = unpacked(around(packed(state[:, :, B - REACH :]), "ocn", 1))
    after = unpacked(around(packed(state[:, :, :REACH]), "ocn", -1))
    before = jnp.where(column > 0, before, 0.0)
    after = jnp.where(column < ocn - 1, after, 0.0)
    gap = jnp.zeros((4, CX, B - 2 * REACH), jnp.float32)
    state = jnp.concatenate([state, after, gap, before], axis=2)

    flux, wide, to_pair, to_beside = sum_rows(arrived, state, devices)
    pair = with_pair(to_pair)
    beside = with_beside(to_beside)
    return substeps(lines, state, flux, wide, pair, beside, state_pair, state_beside)


def solution(mesh):
    mesh = Mesh(mesh.devices.reshape(SIZES), AXES)
    cells = P(ATM, "ocn")
    placed = (
        P(None, AXES),
        P(AXES, None, None),
        P(AXES),
        P(AXES, None),
        P(AXES),
        cells,
        cells,
        cells,
        cells,
    )
    return jax.shard_map(
        on_device,
        mesh=mesh,
        in_specs=placed,
        out_specs=(P(None, ATM, "ocn"), cells, cells, cells),
        check_vma=False,
    )
```
